128 devices in a mesh: tile: 16 (over y, x_lo, core), lat: 8 (over x_hi, z).
Axes of the slice: x: 4 (x_hi: 2, x_lo: 2; x = x_hi * 2 + x_lo), y: 4, z: 4, core: 2. Of those that a mesh axis runs over, the one named last changes fastest.
Arguments:
- field: bfloat16 [384, 768, 256], P('lat', 'tile'), may hold values from -6 to 6
- cotangent: bfloat16 [384, 768, 256], P('lat', 'tile'), may hold values from -9 to 9
- first_weight: bfloat16 [3, 3, 256, 256], replicated, may hold values from -0.125 to 0.125
- second_weight: bfloat16 [3, 3, 256, 256], replicated, may hold values from -0.125 to 0.125
- side_links: int32 [8, 16, 4, 3], replicated, may hold values from 0 to 7, as said below
- corner_links: int32 [8, 16, 4, 3], replicated, may hold values from 0 to 8, as said below
Outputs:
- mixed: bfloat16 [384, 768, 256], P('lat', 'tile')
- input_grad: bfloat16 [384, 768, 256], P('lat', 'tile')
- first_weight_grad: float32 [3, 3, 256, 256], replicated
- second_weight_grad: float32 [3, 3, 256, 256], replicated
The draws below stay inside these ranges and needn't reach their ends.
Inputs may be any that keep to these rules, and one draw needn't show every extreme that they name: `side_links`: entry [i, j, s] describes side s of tile (i, j) in that tile's frame (0 row above, 1 row below, 2 column left, 3 column right): [0] the slot of the neighbouring tile, [1] which of its edges fills the strip, [2] 1 where the strip runs in reverse order, else 0. The tiles' frames are quarter-turn rotations of one grid that wraps both ways, so each edge of a tile fills exactly one strip of one side neighbour. `corner_links`: entry [i, j, c] describes padded corner c of tile (i, j): [0] the slot of the diagonal neighbour, [1] which of its corners, [2] 1 where the padded corner is kept and 0 where it is missing. Each corner of a tile is named by exactly one diagonal neighbour.
All inputs are finite; a program needn't handle non-finite values.
Results may differ from the reference program's by a relative error of at most 0.0085.
Values may be sent and summed in bfloat16 or wider, within the bound.
No kernel may reach another device: no remote copies, remote signals or barrier semaphores. Data moves between devices by JAX's collectives and lax.ppermute only.
A program may use at most 192 MiB of HBM per device.

```python
import math
import jax
import jax.numpy as jnp
from jax import lax

S = 48
C = 256
LAT_CELLS = 384
LON_CELLS = 768
N_TILE = 16
N_LAT = 8


def tile_links(key):
    lat_count = N_LAT
    lon_count = N_TILE
    tile_count = lat_count * lon_count
    turn_count = jax.random.randint(jax.random.fold_in(key, 101), (tile_count,), 0, 4)
    keep_flag = jnp.where(jax.random.randint(jax.random.fold_in(key, 102), (tile_count, 4), 0, 4) == 0, 0, 1).astype(jnp.int32)
    row_ids = jnp.arange(2 * lat_count, dtype=jnp.int32)[:, None]
    col_ids = jnp.arange(2 * lon_count, dtype=jnp.int32)[None, :]
    labels = (row_ids // 2 * lon_count + col_ids // 2) * 4 + row_ids % 2 * 2 + col_ids % 2
    framed = jnp.pad(labels, 1, mode='wrap')
    tile_ids = jnp.arange(tile_count, dtype=jnp.int32)
    lat_of = tile_ids // lon_count
    lon_of = tile_ids % lon_count
    windows = jax.vmap(lambda row_at, col_at: lax.dynamic_slice(framed, (2 * row_at, 2 * col_at), (4, 4)))(lat_of, lon_of)
    turned = jnp.stack([jnp.rot90(windows, k, axes=(1, 2)) for k in range(4)])
    choose = (turn_count[None, :] == jnp.arange(4)[:, None]).astype(jnp.int32)[:, :, None, None]
    local_frame = jnp.sum(turned * choose, axis=0)
    inner_ids = local_frame[:, 1:3, 1:3]
    edge_ids = jnp.stack([inner_ids[:, 0, :], inner_ids[:, 1, :], inner_ids[:, :, 0], inner_ids[:, :, 1]], axis=1)
    corner_ids = jnp.stack([inner_ids[:, 0, 0], inner_ids[:, 0, 1], inner_ids[:, 1, 0], inner_ids[:, 1, 1]], axis=1)
    strips = jnp.stack([local_frame[:, 0, 1:3], local_frame[:, 3, 1:3], local_frame[:, 1:3, 0], local_frame[:, 1:3, 3]], axis=1)
    frame_corners = jnp.stack([local_frame[:, 0, 0], local_frame[:, 0, 3], local_frame[:, 3, 0], local_frame[:, 3, 3]], axis=1)

    def slot_of(source_ids):
        lat_step = (lat_of[source_ids] - lat_of[:, None] + 1) % lat_count
        lon_step = (lon_of[source_ids] - lon_of[:, None] + 1) % lon_count
        return lat_step * 3 + lon_step
    source_ids = strips[:, :, 0] // 4
    candidates = edge_ids[source_ids]
    same_order = jnp.all(candidates == strips[:, :, None, :], axis=-1)
    flipped = jnp.all(candidates == strips[:, :, None, ::-1], axis=-1)
    edge_pick = jnp.argmax((same_order | flipped).astype(jnp.int32), axis=-1)
    flip_flag = jnp.take_along_axis(flipped, edge_pick[..., None], axis=-1)[..., 0].astype(jnp.int32)
    side_links = jnp.stack([slot_of(source_ids), edge_pick, flip_flag], axis=-1).astype(jnp.int32)
    corner_source = frame_corners // 4
    corner_pick = jnp.argmax((corner_ids[corner_source] == frame_corners[:, :, None]).astype(jnp.int32), axis=-1)
    corner_links = jnp.stack([slot_of(corner_source), corner_pick, keep_flag], axis=-1).astype(jnp.int32)
    return (side_links.reshape(lat_count, lon_count, 4, 3), corner_links.reshape(lat_count, lon_count, 4, 3))


def draw_side_links(key, part):
    shared = tile_links(key)
    return shared[0]


def draw_corner_links(key, part):
    shared = tile_links(key)
    return shared[1]


def draw_cotangent(key, part):
    key = jax.random.fold_in(key, 7)
    lat_tile = jnp.arange(N_LAT * S) // S
    lon_tile = jnp.arange(N_TILE * S) // S
    order = (lat_tile[:, None] * N_TILE + lon_tile[None, :]).astype(jnp.float32) / (N_LAT * N_TILE - 1)
    growth = jnp.exp(order * math.log(3.0))[:, :, None]
    base = jnp.clip(jax.random.normal(key, (N_LAT * S, N_TILE * S, C), jnp.float32), -3.0, 3.0)
    return (base * growth).astype(jnp.bfloat16)


def shard_levels(key, extent, shards, smallest, high):
    def one(dim, shards_of):
        steps = jax.random.uniform(jax.random.fold_in(jax.random.fold_in(key, 6), dim), (shards_of,), jnp.float32, smallest / len(shards), high / len(shards))
        return jnp.repeat(jnp.exp(steps), extent[dim] // shards_of).reshape((-1,) + (1,) * (len(extent) - dim - 1))

    factor_of = one(*shards[0])
    for cut in shards[1:]:
        factor_of = factor_of * one(*cut)
    return factor_of


def normal_values(stream_key, shape, width, limit, split=(), held_as=jnp.bfloat16):
    loudness = shard_levels(stream_key, shape, split, -0.22, 0.18) if split else 1.0
    array = jax.random.normal(stream_key, shape, jnp.float32) * width * loudness
    return jnp.minimum(jnp.maximum(array, -limit), limit).astype(held_as)


def setup_inputs(seed: int = 0) -> dict:
    key_list = jax.random.split(jax.random.key(seed), 7)
    field = normal_values(key_list[0], (LAT_CELLS, LON_CELLS, C), 1.0, 6.0, ((0, 8), (1, 16)))
    cotangent = draw_cotangent(jax.random.fold_in(key_list[6], 71), 0)
    first_weight = normal_values(key_list[2], (3, 3, C, C), (9 * C) ** -0.5, 0.125)
    second_weight = normal_values(key_list[3], (3, 3, C, C), (9 * C) ** -0.5, 0.125)
    side_links = draw_side_links(jax.random.fold_in(key_list[6], 71), 0)
    corner_links = draw_corner_links(jax.random.fold_in(key_list[6], 71), 0)
    return {"field": field, "cotangent": cotangent, "first_weight": first_weight, "second_weight": second_weight, "side_links": side_links, "corner_links": corner_links}


def gelu(values):
    return jax.nn.gelu(values, approximate=False)

def gelu_slope(values):
    return jax.jvp(gelu, (values,), (jnp.ones_like(values),))[1]

def split_tiles(whole):
    return whole.reshape(N_LAT, S, N_TILE, S, C).transpose(0, 2, 1, 3, 4)

def join_tiles(parts):
    return parts.transpose(0, 2, 1, 3, 4).reshape(N_LAT * S, N_TILE * S, C)

def source_tiles(slots):
    lat_ids = jnp.arange(N_LAT, dtype=jnp.int32)[:, None, None]
    lon_ids = jnp.arange(N_TILE, dtype=jnp.int32)[None, :, None]
    return ((lat_ids + slots // 3 - 1) % N_LAT * N_TILE + (lon_ids + slots % 3 - 1) % N_TILE).astype(jnp.int32)

def pad_all(parts, side_links, corner_links):
    edge_rows = jnp.stack([parts[:, :, 0], parts[:, :, -1], parts[:, :, :, 0], parts[:, :, :, -1]], axis=2)
    corner_vals = jnp.stack([parts[:, :, 0, 0], parts[:, :, 0, -1], parts[:, :, -1, 0], parts[:, :, -1, -1]], axis=2)
    flat_edges = edge_rows.reshape(N_LAT * N_TILE * 4, S, C)
    flat_corners = corner_vals.reshape(N_LAT * N_TILE * 4, C)
    pick = (source_tiles(side_links[..., 0]) * 4 + side_links[..., 1]).astype(jnp.int32)
    strips = flat_edges[pick]
    flip_flag = (side_links[..., 2] == 1)[..., None, None]
    strips = jnp.where(flip_flag, strips[:, :, :, ::-1], strips)
    corner_pick = (source_tiles(corner_links[..., 0]) * 4 + corner_links[..., 1]).astype(jnp.int32)
    cells = flat_corners[corner_pick] * corner_links[..., 2][..., None].astype(parts.dtype)
    middle = jnp.concatenate([strips[:, :, 2][:, :, :, None, :], parts, strips[:, :, 3][:, :, :, None, :]], axis=3)
    upper = jnp.concatenate([cells[:, :, 0][:, :, None, :], strips[:, :, 0], cells[:, :, 1][:, :, None, :]], axis=2)
    lower = jnp.concatenate([cells[:, :, 2][:, :, None, :], strips[:, :, 1], cells[:, :, 3][:, :, None, :]], axis=2)
    return jnp.concatenate([upper[:, :, None], middle, lower[:, :, None]], axis=2)

def conv_all(framed, weight):
    count = N_LAT * N_TILE * S * S
    total = jnp.zeros((count, C), jnp.float32)
    for a in range(3):
        for b in range(3):
            window = framed[:, :, a:a + S, b:b + S].reshape(count, C)
            total = total + jnp.dot(window, weight[a, b], preferred_element_type=jnp.float32)
    return total

def kernel_total(framed, delta):
    count = N_LAT * N_TILE * S * S
    blocks = []
    for a in range(3):
        for b in range(3):
            window = framed[:, :, a:a + S, b:b + S].reshape(count, C)
            blocks.append(jnp.dot(window.T, delta, preferred_element_type=jnp.float32))
    return jnp.stack(blocks).reshape(3, 3, C, C)

def spread_all(delta, weight):
    total = jnp.zeros((N_LAT, N_TILE, S + 2, S + 2, C), jnp.float32)
    for a in range(3):
        for b in range(3):
            part = jnp.dot(delta, weight[a, b].T, preferred_element_type=jnp.float32).reshape(N_LAT, N_TILE, S, S, C)
            total = total + jnp.pad(part, ((0, 0), (0, 0), (a, 2 - a), (b, 2 - b), (0, 0)))
    return total

def round_rim(framed):
    cycle = jnp.ones((S + 2, S + 2), bool).at[1:-1, 1:-1].set(False)[:, :, None]
    rounded = lax.optimization_barrier(framed.astype(jnp.bfloat16)).astype(jnp.float32)
    return jnp.where(cycle, rounded, framed)

def pull_back(framed, side_links, corner_links):
    start = jnp.zeros((N_LAT, N_TILE, S, S, C), jnp.float32)
    _, transpose_fn = jax.vjp(lambda parts: pad_all(parts, side_links, corner_links), start)
    return transpose_fn(round_rim(framed))[0]

def reference(field, cotangent, first_weight, second_weight, side_links, corner_links):
    count = N_LAT * N_TILE * S * S
    first_frame = pad_all(split_tiles(field), side_links, corner_links)
    first_sum = conv_all(first_frame, first_weight)
    hidden = gelu(first_sum).astype(jnp.bfloat16)
    second_frame = pad_all(hidden.reshape(N_LAT, N_TILE, S, S, C), side_links, corner_links)
    second_sum = conv_all(second_frame, second_weight)
    mixed = gelu(second_sum).astype(jnp.bfloat16)
    upstream = split_tiles(cotangent).reshape(count, C).astype(jnp.float32)
    second_delta = (upstream * gelu_slope(second_sum)).astype(jnp.bfloat16)
    second_total = kernel_total(second_frame, second_delta)
    hidden_grad = pull_back(spread_all(second_delta, second_weight), side_links, corner_links)
    first_delta = (hidden_grad.reshape(count, C) * gelu_slope(first_sum)).astype(jnp.bfloat16)
    first_total = kernel_total(first_frame, first_delta)
    input_grad = pull_back(spread_all(first_delta, first_weight), side_links, corner_links)
    root = math.sqrt(N_LAT * N_TILE * S * S)
    mixed_out = join_tiles(mixed.reshape(N_LAT, N_TILE, S, S, C))
    grad_out = join_tiles(input_grad).astype(jnp.bfloat16)
    return (mixed_out, grad_out, first_total / root, second_total / root)
```

```python
import functools
import math

import jax
import jax.numpy as jnp
from jax import lax
from jax.experimental import pallas as pl
from jax.experimental.pallas import tpu as pltpu
from jax.sharding import PartitionSpec as P

S = 48
C = 256
CELLS = S * S
ROWS = 8
BLK = ROWS * S
N_BLK = S // ROWS
PK = 64
F32 = jnp.float32
BF = jnp.bfloat16
MIB = 1 << 20


def side_slot(lk, s):
    return lk[s * 3]


def side_flip(lk, s):
    return lk[s * 3 + 2]


def corner_slot(lk, c):
    return lk[12 + c * 3]


def corner_keep(lk, c):
    return lk[12 + c * 3 + 2]


def side_facing(lk, slot):
    found = jnp.int32(0)
    for s in range(1, 4):
        found = jnp.where(side_slot(lk, s) == slot, jnp.int32(s), found)
    return found


def flip_facing(lk, slot):
    found = side_flip(lk, 0)
    for s in range(1, 4):
        found = jnp.where(side_slot(lk, s) == slot, side_flip(lk, s), found)
    return found


def corner_facing(lk, slot, values):
    found = values[0]
    for c in range(1, 4):
        found = jnp.where(corner_slot(lk, c) == slot, values[c], found)
    return found


def corner_home(lk, c):
    d = corner_slot(lk, c)
    home = jnp.where(d == 0, jnp.int32(S), jnp.int32(S + 1))
    home = jnp.where(d == 6, jnp.int32(3 * PK + S), home)
    return jnp.where(d == 8, jnp.int32(3 * PK + S + 1), home)


def side_home(lk, s):
    return (side_slot(lk, s) - 1) // 2 * PK


def grid_of(rows, cols):
    row = lax.broadcasted_iota(jnp.int32, (rows, cols), 0)
    col = lax.broadcasted_iota(jnp.int32, (rows, cols), 1)
    return row, col


def ones_at(hit):
    return jnp.where(hit, 1.0, 0.0).astype(BF)


def pick(hit, rows):
    return jnp.dot(ones_at(hit), rows, preferred_element_type=F32)


CORNERS_TO_SEND = {1: (0, 6), 2: (2, 8)}


def pack_edges(lk, edges):
    row, col = grid_of(PK, 4 * S)
    at = [jnp.int32(c // 2 * S + c % 2 * (S - 1)) for c in range(4)]
    hits = []
    for q, slot in enumerate((1, 3, 5, 7)):
        want = jnp.where(row < S, side_facing(lk, slot) * S + row, -1)
        if q in CORNERS_TO_SEND:
            for k, far in enumerate(CORNERS_TO_SEND[q]):
                want = jnp.where(row == S + k, corner_facing(lk, far, at), want)
        hits.append(col == want)
    return pick(jnp.concatenate(hits, axis=0), edges).astype(BF)


def pack_rims(lk, rims):
    row, col = grid_of(PK, 4 * PK)
    at = []
    for c in range(4):
        place = jnp.int32(c // 2 * PK + S + c % 2)
        at.append(jnp.where(corner_keep(lk, c) != 0, place, jnp.int32(-1)))
    hits = []
    for q, slot in enumerate((1, 3, 5, 7)):
        cell = jnp.where(flip_facing(lk, slot) == 1, S - 1 - row, row)
        want = jnp.where(row < S, side_facing(lk, slot) * PK + cell, -1)
        if q in CORNERS_TO_SEND:
            for k, far in enumerate(CORNERS_TO_SEND[q]):
                want = jnp.where(row == S + k, corner_facing(lk, far, at), want)
        hits.append(col == want)
    return pick(jnp.concatenate(hits, axis=0), rims).astype(BF)


def halo_rows(lk, got):
    row, col = grid_of(S, 4 * PK)
    sides = []
    for s in range(4):
        taps = []
        for t in range(3):
            at = row + (t - 1)
            cell = jnp.where(side_flip(lk, s) == 1, S - 1 - at, at)
            want = jnp.where((at >= 0) & (at < S), side_home(lk, s) + cell, -1)
            if s < 2:
                for end, c in ((-1, 2 * s), (S, 2 * s + 1)):
                    home = jnp.where(corner_keep(lk, c) != 0, corner_home(lk, c), -1)
                    want = jnp.where(at == end, home, want)
            taps.append(pick(col == want, got).astype(BF))
        sides.append(jnp.concatenate(taps, axis=1))
    return sides


def rim_adds(lk, got):
    row, col = grid_of(S, 4 * PK)
    adds = []
    for s in range(4):
        hit = col == side_home(lk, s) + row
        if s < 2:
            for end, c in ((0, 2 * s), (S - 1, 2 * s + 1)):
                hit = hit | ((row == end) & (col == corner_home(lk, c)))
        adds.append(pick(hit, got))
    return adds


def cross(adds):
    top, bottom, left, right = adds
    row = lax.broadcasted_iota(jnp.int32, (S, C), 0)
    first = row == 0
    last = row == S - 1

    def with_ends(base, head, tail):
        return base + jnp.where(first, head, 0.0) + jnp.where(last, tail, 0.0)

    return [
        with_ends(top, left[0:1], right[0:1]),
        with_ends(bottom, left[S - 1 :], right[S - 1 :]),
        with_ends(left, top[0:1], bottom[0:1]),
        with_ends(right, top[S - 1 :], bottom[S - 1 :]),
    ]


def gelu_both(z):
    phi = 0.5 + 0.5 * lax.erf(z * (1.0 / math.sqrt(2.0)))
    dens = jnp.exp(z * z * -0.5) * (1.0 / math.sqrt(2.0 * math.pi))
    return z * phi, phi + z * dens


def dot(a, b):
    return jnp.dot(a, b, preferred_element_type=F32)


def dot_nt(a, b):
    return lax.dot_general(a, b, (((1,), (1,)), ((), ())), preferred_element_type=F32)


def halo_sums(sides, w):
    out = [dot(sides[0], w[0]), dot(sides[1], w[2])]
    for s, b in ((2, 0), (3, 2)):
        total = None
        for a in range(3):
            term = dot(sides[s][:, a * C : (a + 1) * C], w[a, b * C : (b + 1) * C])
            total = term if total is None else total + term
        out.append(total)
    return cross(out)


def rims_of(edges, w):
    row, col = grid_of(PK, 4 * S)
    out = []
    for s in range(4):
        total = None
        for t in range(3):
            if s < 2:
                pos = jnp.where(row < S, row + 1, jnp.where(row == S, 0, S + 1))
                used = row < S + 2
                a, b = (0, 2)[s], t
            else:
                pos = row + 1
                used = row < S
                a, b = t, (0, 2)[s - 2]
            src = pos - t
            hit = used & (src >= 0) & (src < S) & (col == s * S + src)
            term = dot_nt(pick(hit, edges).astype(BF), w[a, b * C : (b + 1) * C])
            total = term if total is None else total + term
        out.append(total.astype(BF))
    return jnp.concatenate(out, axis=0)


def put_edges(x, edges):
    x[pl.ds(0, S)] = edges[pl.ds(0, S)]
    x[pl.ds(CELLS - S, S)] = edges[pl.ds(S, S)]
    for r in range(S):
        x[pl.ds(r * S, 1)] = edges[pl.ds(2 * S + r, 1)]
        x[pl.ds(r * S + S - 1, 1)] = edges[pl.ds(3 * S + r, 1)]


def take_edges(x, edges):
    edges[pl.ds(0, S)] = x[pl.ds(0, S)]
    edges[pl.ds(S, S)] = x[pl.ds(CELLS - S, S)]
    for r in range(S):
        edges[pl.ds(2 * S + r, 1)] = x[pl.ds(r * S, 1)]
        edges[pl.ds(3 * S + r, 1)] = x[pl.ds(r * S + S - 1, 1)]


def spread_columns(x, frame, left, right):
    zero = jnp.zeros((S, 3 * C), BF)
    frame[pl.ds(0, S)] = zero
    frame[pl.ds(CELLS + S, S)] = zero
    row = lax.broadcasted_iota(jnp.int32, (S, C), 0)

    @pl.loop(0, S, unroll=4)
    def _(r):
        cells = x[pl.ds(pl.multiple_of(r * S, S), S)]
        to = pl.ds(pl.multiple_of(r * S + S, S), S)
        before = jnp.where(row == 0, 0.0, pltpu.roll(cells, 1, 0))
        after = jnp.where(row == S - 1, 0.0, pltpu.roll(cells, S - 1, 0))
        frame[to, left * C : (left + 1) * C] = before.astype(BF)
        frame[to, C : 2 * C] = cells.astype(BF)
        frame[to, right * C : (right + 1) * C] = after.astype(BF)


def block_of(i):
    return pl.ds(pl.multiple_of(i * BLK, BLK), BLK)


def conv_block(frame, w, i):
    total = None
    for a in range(3):
        term = dot(frame[pl.ds(pl.multiple_of(i * BLK + a * S, S), BLK)], w[a])
        total = term if total is None else total + term
    return total


def back_block(frame, w, i):
    total = None
    for a in range(3):
        at = pl.ds(pl.multiple_of(i * BLK + (2 - a) * S, S), BLK)
        for b in range(3):
            part = frame[at, b * C : (b + 1) * C]
            term = dot_nt(part, w[a, b * C : (b + 1) * C])
            total = term if total is None else total + term
    return total


def weight_sums(xt, frame, halo, edges, out):
    side = []
    for s in range(4):
        side.append(
            lax.dot_general(
                halo[s * S : (s + 1) * S],
                edges[s * S : (s + 1) * S],
                (((0,), (0,)), ((), ())),
                preferred_element_type=F32,
            )
        )
    for a in range(3):
        whole = dot(xt[...], frame[pl.ds((2 - a) * S, CELLS)])
        for b in range(3):
            part = whole[:, b * C : (b + 1) * C]
            if a == 0:
                part = part + side[0][b * C : (b + 1) * C]
            if a == 2:
                part = part + side[1][b * C : (b + 1) * C]
            if b == 0:
                part = part + side[2][a * C : (a + 1) * C]
            if b == 2:
                part = part + side[3][a * C : (a + 1) * C]
            out[pl.ds((a * 3 + b) * C, C)] = part.astype(out.dtype)


def k_pack_field(lk, field, pk):
    def edge_column(at):
        lo = at // 16 * 16
        part = field[:, lo : lo + 16, :].astype(F32)
        row = lax.broadcasted_iota(jnp.int32, (S, 16, C), 1)
        return jnp.sum(jnp.where(row == at - lo, part, 0.0), axis=1)

    edges = jnp.concatenate(
        [field[0], field[S - 1], edge_column(0).astype(BF), edge_column(S - 1).astype(BF)],
        axis=0,
    )
    pk[...] = pack_edges(lk, edges)


def k_first(field, w, hidden, slope, e0, xt, x, frame):
    x[...] = field[...].astype(F32)
    spread_columns(x, frame, 0, 2)
    xt[...] = field[...].T

    @pl.loop(0, N_BLK)
    def _(i):
        at = block_of(i)
        z = conv_block(frame, w, i)
        x[at] = z
        value, grad = gelu_both(z)
        hidden[at] = value.astype(BF)
        slope[at] = grad

    take_edges(x, e0)


def join(got):
    return jnp.concatenate([g[...] for g in got], axis=0)


def k_first_edges(lk, up, left, right, down, e0, w, halo, slope, hidden, pk):
    sides = halo_rows(lk, join((up, left, right, down)))
    for s in range(4):
        halo[pl.ds(s * S, S)] = sides[s]
    z = e0[...] + jnp.concatenate(halo_sums(sides, w), axis=0)
    value, grad = gelu_both(z)
    slope[...] = grad
    hidden[...] = value.astype(BF)
    pk[...] = pack_edges(lk, value.astype(BF))


def k_second(hidden0, he, cot, w, xt, mixed, delta, e0, ec, x, frame, edges):
    x[...] = cot[...].astype(F32)
    take_edges(x, ec)
    x[...] = hidden0[...].astype(F32)
    edges[...] = he[...].astype(F32)
    put_edges(x, edges)
    spread_columns(x, frame, 0, 2)
    xt[...] = x[...].astype(BF).T

    @pl.loop(0, N_BLK)
    def _(i):
        at = block_of(i)
        z = conv_block(frame, w, i)
        x[at] = z
        value, grad = gelu_both(z)
        mixed[at] = value.astype(BF)
        delta[at] = (cot[at].astype(F32) * grad).astype(BF)

    take_edges(x, e0)


def k_second_edges(lk, up, left, right, down, e0, ec, w, halo, mixed, delta, pk):
    sides = halo_rows(lk, join((up, left, right, down)))
    for s in range(4):
        halo[pl.ds(s * S, S)] = sides[s]
    z = e0[...] + jnp.concatenate(halo_sums(sides, w), axis=0)
    value, grad = gelu_both(z)
    mixed[...] = value.astype(BF)
    edges = (ec[...] * grad).astype(BF)
    delta[...] = edges
    pk[...] = pack_rims(lk, rims_of(edges, w))


def k_second_back(mixed0, me, delta0, de, w, xt, halo, slope, mixed, total, fd, e0, x, frame, edges):
    x[...] = mixed0[...].astype(F32)
    edges[...] = me[...].astype(F32)
    put_edges(x, edges)
    mixed[...] = x[...].astype(BF)
    x[...] = delta0[...].astype(F32)
    edges[...] = de[...].astype(F32)
    put_edges(x, edges)
    spread_columns(x, frame, 2, 0)

    @pl.loop(0, N_BLK)
    def _(i):
        at = block_of(i)
        g = back_block(frame, w, i)
        x[at] = g
        fd[at] = (g * slope[at]).astype(BF)

    take_edges(x, e0)
    weight_sums(xt, frame, halo, de, total)


def k_first_delta_edges(lk, up, left, right, down, e0, slope, w, delta, pk):
    adds = cross(rim_adds(lk, join((up, left, right, down))))
    grad = e0[...] + jnp.concatenate(adds, axis=0)
    edges = (grad * slope[...]).astype(BF)
    delta[...] = edges
    pk[...] = pack_rims(lk, rims_of(edges, w))


def k_first_total(delta0, de, xt, halo, total, x, frame, edges):
    x[...] = delta0[...].astype(F32)
    edges[...] = de[...].astype(F32)
    put_edges(x, edges)
    spread_columns(x, frame, 2, 0)
    weight_sums(xt, frame, halo, de, total)


def k_input_grad(lk, up, left, right, down, delta0, de, w, out, x, frame, edges):
    x[...] = delta0[...].astype(F32)
    edges[...] = de[...].astype(F32)
    put_edges(x, edges)
    spread_columns(x, frame, 2, 0)

    @pl.loop(0, N_BLK)
    def _(i):
        x[block_of(i)] = back_block(frame, w, i)

    adds = cross(rim_adds(lk, join((up, left, right, down))))
    take_edges(x, edges)
    edges[...] += jnp.concatenate(adds, axis=0)
    put_edges(x, edges)
    out[...] = x[...].astype(BF)


VMEM = pl.BlockSpec(memory_space=pltpu.VMEM)
SMEM = pl.BlockSpec(memory_space=pltpu.SMEM)
WIDE = [pltpu.VMEM((CELLS, C), F32), pltpu.VMEM((CELLS + 2 * S, 3 * C), BF)]
WIDER = WIDE + [pltpu.VMEM((4 * S, C), F32)]


def call(kernel, args, outs, scratch=(), links=None, flops=0):
    given = ([links] if links is not None else []) + list(args)
    specs = ([SMEM] if links is not None else []) + [VMEM] * len(args)
    return pl.pallas_call(
        kernel,
        out_shape=[jax.ShapeDtypeStruct(shape, dtype) for shape, dtype in outs],
        in_specs=specs,
        out_specs=[VMEM] * len(outs),
        scratch_shapes=list(scratch),
        compiler_params=pltpu.CompilerParams(vmem_limit_bytes=40 * MIB),
        cost_estimate=pl.CostEstimate(
            flops=int(flops), bytes_accessed=4 * MIB, transcendentals=0
        ),
        name=kernel.__name__,
    )(*given)


def ring(count, step):
    return [(i, (i + step) % count) for i in range(count)]


def trade(pk):
    n_tile = lax.axis_size("tile")
    n_lat = lax.axis_size("lat")
    up, left, right, down = (pk[q * PK : (q + 1) * PK] for q in range(4))
    from_left = lax.ppermute(right, "tile", ring(n_tile, 1))
    from_right = lax.ppermute(left, "tile", ring(n_tile, -1))
    filler = jnp.zeros((PK - S - 2, C), BF)
    up = jnp.concatenate(
        [up[:S], from_left[S : S + 1], from_right[S : S + 1], filler], axis=0
    )
    down = jnp.concatenate(
        [down[:S], from_left[S + 1 : S + 2], from_right[S + 1 : S + 2], filler], axis=0
    )
    from_up = lax.ppermute(down, "lat", ring(n_lat, 1))
    from_down = lax.ppermute(up, "lat", ring(n_lat, -1))
    return from_up, from_left, from_right, from_down


def group_ring(kind, step):
    pairs = []
    for t in range(16):
        for l in range(8):
            y, xl, c, xh, z = t // 4, t // 2 % 2, t % 2, l // 4, l % 4
            x = xh * 2 + xl
            if kind == "core":
                c = (c + step) % 2
            elif kind == "z":
                z = (z + step) % 4
            elif kind == "y":
                y = (y + step) % 4
            else:
                x = (x + step) % 4
            to = (y * 4 + x % 2 * 2 + c) * 8 + x // 2 * 4 + z
            pairs.append((t * 8 + l, to))
    return pairs


def move(x, kind, step):
    return lax.ppermute(x, ("tile", "lat"), group_ring(kind, step))


def scatter4(x, kind, place):
    k = x.shape[0] // 4
    got = [
        move(lax.dynamic_slice_in_dim(x, (place + s) % 4 * k, k, 0), kind, s) for s in (1, 3, 2)
    ]
    total = lax.dynamic_slice_in_dim(x, place * k, k, 0).astype(F32)
    for g in got:
        total = total + g.astype(F32)
    return total.astype(BF)


def gather4(x, kind, place):
    k = x.shape[0]
    out = jnp.zeros((4 * k, C), x.dtype)
    parts = [(0, x)] + [(s, move(x, kind, 4 - s)) for s in (1, 3, 2)]
    for s, part in parts:
        out = lax.dynamic_update_slice_in_dim(out, part, (place + s) % 4 * k, 0)
    return out


def sum_all(first, second, root):
    tile_at = lax.axis_index("tile")
    lat_at = lax.axis_index("lat")
    core, z_at, y_at = tile_at % 2, lat_at % 4, tile_at // 4
    keep = jnp.where(core == 0, first, second)
    send = jnp.where(core == 0, second, first)
    part = (keep.astype(F32) + move(send, "core", 1).astype(F32)).astype(BF)
    part = scatter4(part, "z", z_at)
    part = scatter4(part, "y", y_at)
    total = part.astype(F32)
    for s in (1, 3, 2):
        total = total + move(part, "x", s).astype(F32)
    part = (total * (1.0 / root)).astype(BF)
    part = gather4(part, "y", y_at)
    part = gather4(part, "z", z_at)
    other = move(part, "core", 1)
    return (
        jnp.where(core == 0, part, other).astype(F32),
        jnp.where(core == 0, other, part).astype(F32),
    )


def shards(field, cotangent, first_weight, second_weight, side_links, corner_links):
    lat_at = lax.axis_index("lat")
    lon_at = lax.axis_index("tile")
    lk = jnp.concatenate(
        [side_links[lat_at, lon_at].reshape(12), corner_links[lat_at, lon_at].reshape(12)]
    )
    w1 = first_weight.reshape(3, 3 * C, C)
    w2 = second_weight.reshape(3, 3 * C, C)
    cells = field.reshape(CELLS, C)
    cot = cotangent.reshape(CELLS, C)
    cell_bf, cell_f32 = ((CELLS, C), BF), ((CELLS, C), F32)
    edge_bf, edge_f32 = ((4 * S, C), BF), ((4 * S, C), F32)
    halo_bf, turned, packs = ((4 * S, 3 * C), BF), ((C, CELLS), BF), ((4 * PK, C), BF)
    work = 2 * CELLS * 9 * C * C

    (pk,) = call(k_pack_field, [field], [packs], links=lk)
    got = trade(pk)
    hidden0, slope0, e0, xt1 = call(
        k_first, [cells, w1], [cell_bf, cell_f32, edge_f32, turned], WIDE, flops=work
    )
    halo1, slope_e, hidden_e, pk = call(
        k_first_edges, [*got, e0, w1], [halo_bf, edge_f32, edge_bf, packs], links=lk
    )
    got = trade(pk)
    xt2, mixed0, delta0, e0, ec = call(
        k_second,
        [hidden0, hidden_e, cot, w2],
        [turned, cell_bf, cell_bf, edge_f32, edge_f32],
        WIDER,
        flops=work,
    )
    halo2, mixed_e, delta_e, pk = call(
        k_second_edges, [*got, e0, ec, w2], [halo_bf, edge_bf, edge_bf, packs], links=lk
    )
    got = trade(pk)
    mixed, total2, fd0, e0 = call(
        k_second_back,
        [mixed0, mixed_e, delta0, delta_e, w2, xt2, halo2, slope0],
        [cell_bf, cell_bf, cell_bf, edge_f32],
        WIDER,
        flops=2 * work,
    )
    fd_e, pk = call(
        k_first_delta_edges, [*got, e0, slope_e, w1], [edge_bf, packs], links=lk
    )
    got = trade(pk)
    (total1,) = call(
        k_first_total, [fd0, fd_e, xt1, halo1], [cell_bf], WIDER, flops=work
    )
    root = math.sqrt(CELLS * lax.axis_size("lat") * lax.axis_size("tile"))
    first, second = sum_all(total1, total2, root)
    (grad,) = call(
        k_input_grad, [*got, fd0, fd_e, w1], [cell_bf], WIDER, links=lk, flops=work
    )
    return (
        mixed.reshape(S, S, C),
        grad.reshape(S, S, C),
        first.reshape(3, 3, C, C),
        second.reshape(3, 3, C, C),
    )


def solution(mesh):
    placed = (P("lat", "tile", None), P("lat", "tile", None), P(), P(), P(), P())
    return jax.shard_map(
        shards,
        mesh=mesh,
        in_specs=placed,
        out_specs=(P("lat", "tile", None), P("lat", "tile", None), P(), P()),
        check_vma=False,
    )
```

```python
import functools
import math

import jax
import jax.numpy as jnp
from jax import lax
from jax.experimental import pallas as pl
from jax.experimental.pallas import tpu as pltpu
from jax.sharding import PartitionSpec as P

S = 48
C = 256
CELLS = S * S
ROWS = 8
BLK = ROWS * S
N_BLK = S // ROWS
PK = 64
F32 = jnp.float32
BF = jnp.bfloat16
MIB = 1 << 20


def side_slot(lk, s):
    return lk[s * 3]


def side_flip(lk, s):
    return lk[s * 3 + 2]


def corner_slot(lk, c):
    return lk[12 + c * 3]


def corner_keep(lk, c):
    return lk[12 + c * 3 + 2]


def side_facing(lk, slot):
    found = jnp.int32(0)
    for s in range(1, 4):
        found = jnp.where(side_slot(lk, s) == slot, jnp.int32(s), found)
    return found


def flip_facing(lk, slot):
    found = side_flip(lk, 0)
    for s in range(1, 4):
        found = jnp.where(side_slot(lk, s) == slot, side_flip(lk, s), found)
    return found


def corner_facing(lk, slot, values):
    found = values[0]
    for c in range(1, 4):
        found = jnp.where(corner_slot(lk, c) == slot, values[c], found)
    return found


def corner_home(lk, c):
    d = corner_slot(lk, c)
    home = jnp.where(d == 0, jnp.int32(S), jnp.int32(S + 1))
    home = jnp.where(d == 6, jnp.int32(3 * PK + S), home)
    return jnp.where(d == 8, jnp.int32(3 * PK + S + 1), home)


def side_home(lk, s):
    return (side_slot(lk, s) - 1) // 2 * PK


def grid_of(rows, cols):
    row = lax.broadcasted_iota(jnp.int32, (rows, cols), 0)
    col = lax.broadcasted_iota(jnp.int32, (rows, cols), 1)
    return row, col


def ones_at(hit):
    return jnp.where(hit, 1.0, 0.0).astype(BF)


def pick(hit, rows):
    return jnp.dot(ones_at(hit), rows, preferred_element_type=F32)


CORNERS_TO_SEND = {1: (0, 6), 2: (2, 8)}


def pack_edges(lk, edges):
    row, col = grid_of(PK, 4 * S)
    at = [jnp.int32(c // 2 * S + c % 2 * (S - 1)) for c in range(4)]
    hits = []
    for q, slot in enumerate((1, 3, 5, 7)):
        want = jnp.where(row < S, side_facing(lk, slot) * S + row, -1)
        if q in CORNERS_TO_SEND:
            for k, far in enumerate(CORNERS_TO_SEND[q]):
                want = jnp.where(row == S + k, corner_facing(lk, far, at), want)
        hits.append(col == want)
    return pick(jnp.concatenate(hits, axis=0), edges).astype(BF)


def pack_rims(lk, rims):
    row, col = grid_of(PK, 4 * PK)
    at = []
    for c in range(4):
        place = jnp.int32(c // 2 * PK + S + c % 2)
        at.append(jnp.where(corner_keep(lk, c) != 0, place, jnp.int32(-1)))
    hits = []
    for q, slot in enumerate((1, 3, 5, 7)):
        cell = jnp.where(flip_facing(lk, slot) == 1, S - 1 - row, row)
        want = jnp.where(row < S, side_facing(lk, slot) * PK + cell, -1)
        if q in CORNERS_TO_SEND:
            for k, far in enumerate(CORNERS_TO_SEND[q]):
                want = jnp.where(row == S + k, corner_facing(lk, far, at), want)
        hits.append(col == want)
    return pick(jnp.concatenate(hits, axis=0), rims).astype(BF)


def halo_rows(lk, got):
    row, col = grid_of(S, 4 * PK)
    sides = []
    for s in range(4):
        taps = []
        for t in range(3):
            at = row + (t - 1)
            cell = jnp.where(side_flip(lk, s) == 1, S - 1 - at, at)
            want = jnp.where((at >= 0) & (at < S), side_home(lk, s) + cell, -1)
            if s < 2:
                for end, c in ((-1, 2 * s), (S, 2 * s + 1)):
                    home = jnp.where(corner_keep(lk, c) != 0, corner_home(lk, c), -1)
                    want = jnp.where(at == end, home, want)
            taps.append(pick(col == want, got).astype(BF))
        sides.append(jnp.concatenate(taps, axis=1))
    return sides


def rim_adds(lk, got):
    row, col = grid_of(S, 4 * PK)
    adds = []
    for s in range(4):
        hit = col == side_home(lk, s) + row
        if s < 2:
            for end, c in ((0, 2 * s), (S - 1, 2 * s + 1)):
                hit = hit | ((row == end) & (col == corner_home(lk, c)))
        adds.append(pick(hit, got))
    return adds


def cross(adds):
    top, bottom, left, right = adds
    row = lax.broadcasted_iota(jnp.int32, (S, C), 0)
    first = row == 0
    last = row == S - 1

    def with_ends(base, head, tail):
        return base + jnp.where(first, head, 0.0) + jnp.where(last, tail, 0.0)

    return [
        with_ends(top, left[0:1], right[0:1]),
        with_ends(bottom, left[S - 1 :], right[S - 1 :]),
        with_ends(left, top[0:1], bottom[0:1]),
        with_ends(right, top[S - 1 :], bottom[S - 1 :]),
    ]


def gelu_both(z):
    phi = 0.5 + 0.5 * lax.erf(z * (1.0 / math.sqrt(2.0)))
    dens = jnp.exp(z * z * -0.5) * (1.0 / math.sqrt(2.0 * math.pi))
    return z * phi, phi + z * dens


def dot(a, b):
    return jnp.dot(a, b, preferred_element_type=F32)


def dot_nt(a, b):
    return lax.dot_general(a, b, (((1,), (1,)), ((), ())), preferred_element_type=F32)


def halo_sums(sides, w):
    out = [dot(sides[0], w[0]), dot(sides[1], w[2])]
    for s, b in ((2, 0), (3, 2)):
        total = None
        for a in range(3):
            term = dot(sides[s][:, a * C : (a + 1) * C], w[a, b * C : (b + 1) * C])
            total = term if total is None else total + term
        out.append(total)
    return cross(out)


def rims_of(edges, w):
    row, col = grid_of(PK, 4 * S)
    out = []
    for s in range(4):
        total = None
        for t in range(3):
            if s < 2:
                pos = jnp.where(row < S, row + 1, jnp.where(row == S, 0, S + 1))
                used = row < S + 2
                a, b = (0, 2)[s], t
            else:
                pos = row + 1
                used = row < S
                a, b = t, (0, 2)[s - 2]
            src = pos - t
            hit = used & (src >= 0) & (src < S) & (col == s * S + src)
            term = dot_nt(pick(hit, edges).astype(BF), w[a, b * C : (b + 1) * C])
            total = term if total is None else total + term
        out.append(total.astype(BF))
    return jnp.concatenate(out, axis=0)


def put_edges(x, edges):
    x[pl.ds(0, S)] = edges[pl.ds(0, S)]
    x[pl.ds(CELLS - S, S)] = edges[pl.ds(S, S)]
    for r in range(S):
        x[pl.ds(r * S, 1)] = edges[pl.ds(2 * S + r, 1)]
        x[pl.ds(r * S + S - 1, 1)] = edges[pl.ds(3 * S + r, 1)]


def take_edges(x, edges):
    edges[pl.ds(0, S)] = x[pl.ds(0, S)]
    edges[pl.ds(S, S)] = x[pl.ds(CELLS - S, S)]
    for r in range(S):
        edges[pl.ds(2 * S + r, 1)] = x[pl.ds(r * S, 1)]
        edges[pl.ds(3 * S + r, 1)] = x[pl.ds(r * S + S - 1, 1)]


def spread_columns(x, frame, left, right):
    zero = jnp.zeros((S, 3 * C), BF)
    frame[pl.ds(0, S)] = zero
    frame[pl.ds(CELLS + S, S)] = zero
    row = lax.broadcasted_iota(jnp.int32, (S, C), 0)

    @pl.loop(0, S, unroll=4)
    def _(r):
        cells = x[pl.ds(pl.multiple_of(r * S, S), S)]
        to = pl.ds(pl.multiple_of(r * S + S, S), S)
        before = jnp.where(row == 0, 0.0, pltpu.roll(cells, 1, 0))
        after = jnp.where(row == S - 1, 0.0, pltpu.roll(cells, S - 1, 0))
        frame[to, left * C : (left + 1) * C] = before.astype(BF)
        frame[to, C : 2 * C] = cells.astype(BF)
        frame[to, right * C : (right + 1) * C] = after.astype(BF)


def block_of(i):
    return pl.ds(pl.multiple_of(i * BLK, BLK), BLK)


def conv_block(frame, w, i):
    total = None
    for a in range(3):
        term = dot(frame[pl.ds(pl.multiple_of(i * BLK + a * S, S), BLK)], w[a])
        total = term if total is None else total + term
    return total


def back_block(frame, w, i):
    total = None
    for a in range(3):
        at = pl.ds(pl.multiple_of(i * BLK + (2 - a) * S, S), BLK)
        for b in range(3):
            part = frame[at, b * C : (b + 1) * C]
            term = dot_nt(part, w[a, b * C : (b + 1) * C])
            total = term if total is None else total + term
    return total


def weight_sums(xt, frame, halo, edges, store):
    side = []
    for s in range(4):
        side.append(
            lax.dot_general(
                halo[s * S : (s + 1) * S],
                edges[s * S : (s + 1) * S],
                (((0,), (0,)), ((), ())),
                preferred_element_type=F32,
            )
        )
    for a in range(3):
        whole = dot(xt[...], frame[pl.ds((2 - a) * S, CELLS)])
        for b in range(3):
            part = whole[:, b * C : (b + 1) * C]
            if a == 0:
                part = part + side[0][b * C : (b + 1) * C]
            if a == 2:
                part = part + side[1][b * C : (b + 1) * C]
            if b == 0:
                part = part + side[2][a * C : (a + 1) * C]
            if b == 2:
                part = part + side[3][a * C : (a + 1) * C]
            store((a * 3 + b) * C, part.astype(BF))


def edges_of(field):
    def edge_column(at):
        lo = at // 16 * 16
        part = field[:, lo : lo + 16, :].astype(F32)
        row = lax.broadcasted_iota(jnp.int32, (S, 16, C), 1)
        return jnp.sum(jnp.where(row == at - lo, part, 0.0), axis=1)

    return jnp.concatenate(
        [field[0], field[S - 1], edge_column(0).astype(BF), edge_column(S - 1).astype(BF)],
        axis=0,
    )


def k_pack_field(lk, field, pk):
    pk[...] = pack_edges(lk, edges_of(field))


def k_edges(cells, edges):
    edges[...] = edges_of(cells)


def k_first(field, w, after, hidden, slope, e0, xt, x, frame):
    x[...] = field[...].astype(F32)
    xt[...] = field[...].T
    spread_columns(x, frame, 0, 2)

    @pl.loop(0, N_BLK)
    def _(i):
        at = block_of(i)
        z = conv_block(frame, w, i)
        x[at] = z
        value, grad = gelu_both(z)
        hidden[at] = value.astype(BF)
        slope[at] = grad

    take_edges(x, e0)


def join(got):
    return jnp.concatenate([g[...] for g in got], axis=0)


def k_first_edges(lk, up, left, right, down, e0, w, halo, slope, hidden, pk):
    sides = halo_rows(lk, join((up, left, right, down)))
    for s in range(4):
        halo[pl.ds(s * S, S)] = sides[s]
    z = e0[...] + jnp.concatenate(halo_sums(sides, w), axis=0)
    value, grad = gelu_both(z)
    slope[...] = grad
    hidden[...] = value.astype(BF)
    pk[...] = pack_edges(lk, value.astype(BF))


def k_second(he, hidden0, cot, w, after, xt, mixed, delta, e0, x, frame, edges):
    edges[...] = he[...].astype(F32)
    x[...] = hidden0[...].astype(F32)
    put_edges(x, edges)
    xt[...] = x[...].astype(BF).T
    spread_columns(x, frame, 0, 2)

    @pl.loop(0, N_BLK)
    def _(i):
        at = block_of(i)
        z = conv_block(frame, w, i)
        x[at] = z
        value, grad = gelu_both(z)
        mixed[at] = value.astype(BF)
        delta[at] = (cot[at].astype(F32) * grad).astype(BF)

    take_edges(x, e0)


def k_second_edges(lk, up, left, right, down, e0, ec, w, halo, mixed, delta, pk):
    sides = halo_rows(lk, join((up, left, right, down)))
    for s in range(4):
        halo[pl.ds(s * S, S)] = sides[s]
    z = e0[...] + jnp.concatenate(halo_sums(sides, w), axis=0)
    value, grad = gelu_both(z)
    mixed[...] = value.astype(BF)
    edges = (ec[...].astype(F32) * grad).astype(BF)
    delta[...] = edges
    pk[...] = pack_rims(lk, rims_of(edges, w))


def k_second_back(
    de, halo, delta0, w, xt, slope, after, total, fd, e0, x, frame, edges
):
    edges[...] = de[...].astype(F32)
    x[...] = delta0[...].astype(F32)
    put_edges(x, edges)
    spread_columns(x, frame, 2, 0)

    @pl.loop(0, N_BLK)
    def _(i):
        at = block_of(i)
        g = back_block(frame, w, i)
        x[at] = g
        fd[at] = (g * slope[at]).astype(BF)

    take_edges(x, e0)

    def store(row, part):
        total[pl.ds(row, C)] = part

    weight_sums(xt, frame, halo, de, store)


def k_first_delta_edges(lk, up, left, right, down, e0, slope, w, delta, pk):
    adds = cross(rim_adds(lk, join((up, left, right, down))))
    grad = e0[...] + jnp.concatenate(adds, axis=0)
    edges = (grad * slope[...]).astype(BF)
    delta[...] = edges
    pk[...] = pack_rims(lk, rims_of(edges, w))


def k_first_total(at, de, halo, delta0, xt, other, keep, send, x, frame, edges, tv):
    edges[...] = de[...].astype(F32)
    x[...] = delta0[...].astype(F32)
    put_edges(x, edges)
    spread_columns(x, frame, 2, 0)

    def store(row, part):
        tv[pl.ds(row, C)] = part

    weight_sums(xt, frame, halo, de, store)
    here = at[0] == 0
    keep[...] = jnp.where(here, tv[...], other[...])
    send[...] = jnp.where(here, other[...], tv[...])


def k_input_middle(de, delta0, w, after, out, x, frame, edges):
    x[...] = delta0[...].astype(F32)
    edges[...] = de[...].astype(F32)
    put_edges(x, edges)
    spread_columns(x, frame, 2, 0)

    @pl.loop(0, N_BLK)
    def _(i):
        out[block_of(i)] = back_block(frame, w, i)


def k_input_grad(lk, up, left, right, down, middle, mixed0, me, after, out, mixed, x, edges):
    adds = cross(rim_adds(lk, join((up, left, right, down))))
    x[...] = middle[...]
    take_edges(x, edges)
    edges[...] += jnp.concatenate(adds, axis=0)
    put_edges(x, edges)
    out[...] = x[...].astype(BF)
    x[...] = mixed0[...].astype(F32)
    edges[...] = me[...].astype(F32)
    put_edges(x, edges)
    mixed[...] = x[...].astype(BF)


STEPS = (0, 1, 3, 2)


def quarter(place, step, rows):
    return pl.ds(pl.multiple_of((place + step) % 4 * rows, 16), rows)


def k_core_sum(at, keep, got, pk, own, s1, s3, s2, pk_out):
    rows = own.shape[0]
    for step, out in zip(STEPS, (own, s1, s3, s2)):
        part = quarter(at[1], step, rows)
        out[...] = (keep[part].astype(F32) + got[part].astype(F32)).astype(out.dtype)
    pk_out[...] = pk[...]


def k_z_sum(at, own, g1, g3, g2, pk, left, right, after, o, s1, s3, s2, up_out, down_out, x):
    rows = o.shape[0]
    x[...] = (own[...] + g2[...].astype(F32)) + (g1[...].astype(F32) + g3[...].astype(F32))
    for step, out in zip(STEPS, (o, s1, s3, s2)):
        out[...] = x[quarter(at[2], step, rows)].astype(out.dtype)
    up_out[...] = with_corners(pk[0:PK], left[...], right[...], 0)
    down_out[...] = with_corners(pk[3 * PK :], left[...], right[...], 1)


def with_corners(edge, left, right, k):
    row = lax.broadcasted_iota(jnp.int32, (PK, C), 0)
    out = jnp.where(row == S, left[S + k : S + k + 1].astype(F32), edge.astype(F32))
    return jnp.where(row == S + 1, right[S + k : S + k + 1].astype(F32), out).astype(BF)


def k_y_sum(own, g1, g3, g2, out):
    total = (own[...] + g2[...].astype(F32)) + (g1[...].astype(F32) + g3[...].astype(F32))
    out[...] = total.astype(BF)


def k_x_sum(scale, own, g1, g3, g2, out):
    total = (own[...].astype(F32) + g2[...].astype(F32)) + (
        g1[...].astype(F32) + g3[...].astype(F32)
    )
    out[...] = (total * scale).astype(BF)


def k_join(at, own, g1, g3, g2, up, down, out):
    rows = own.shape[0]
    for step, part in zip(STEPS, (own, g1, g3, g2)):
        out[quarter(at[2], step, rows)] = part[...]


def k_unpack(at, a0, a1, a3, a2, b0, b1, b3, b2, after, first, second):
    rows = a0.shape[0]
    here = at[0] == 0
    for step, a, b in zip(STEPS, (a0, a1, a3, a2), (b0, b1, b3, b2)):
        part = quarter(at[1], step, rows)

        @pl.when(here)
        def _():
            first[part] = a[...].astype(F32)
            second[part] = b[...].astype(F32)

        @pl.when(jnp.logical_not(here))
        def _():
            first[part] = b[...].astype(F32)
            second[part] = a[...].astype(F32)


VMEM = pl.BlockSpec(memory_space=pltpu.VMEM)
SMEM = pl.BlockSpec(memory_space=pltpu.SMEM)
ANY = pl.BlockSpec(memory_space=pl.ANY)
CELL_BF = pltpu.VMEM((CELLS, C), BF)
WIDE = [pltpu.VMEM((CELLS, C), F32), pltpu.VMEM((CELLS + 2 * S, 3 * C), BF)]
WIDER = WIDE + [pltpu.VMEM((4 * S, C), F32)]


def call(kernel, args, outs, scratch=(), links=None, flops=0, after=(), limit=8):
    given = ([links] if links is not None else []) + [*args, *after]
    specs = ([SMEM] if links is not None else []) + [VMEM] * len(args)
    specs += [ANY] * len(after)
    name = getattr(kernel, "__name__", "k_x_sum")
    return pl.pallas_call(
        kernel,
        out_shape=[
            (pltpu.VMEM if len(out) > 2 else jax.ShapeDtypeStruct)(out[0], out[1]) for out in outs
        ],
        in_specs=specs,
        out_specs=[VMEM] * len(outs),
        scratch_shapes=list(scratch),
        compiler_params=pltpu.CompilerParams(vmem_limit_bytes=limit * MIB),
        cost_estimate=pl.CostEstimate(
            flops=int(flops), bytes_accessed=4 * MIB, transcendentals=0
        ),
        name=name,
    )(*given)


def ring(count, step):
    return [(i, (i + step) % count) for i in range(count)]


def trade_tile(pk):
    n_tile = lax.axis_size("tile")
    left, right = pk[PK : 2 * PK], pk[2 * PK : 3 * PK]
    from_left = lax.ppermute(right, "tile", ring(n_tile, 1))
    from_right = lax.ppermute(left, "tile", ring(n_tile, -1))
    return from_left, from_right


def trade_lat(up, down):
    n_lat = lax.axis_size("lat")
    from_up = lax.ppermute(down, "lat", ring(n_lat, 1))
    from_down = lax.ppermute(up, "lat", ring(n_lat, -1))
    return from_up, from_down


def trade(pk):
    from_left, from_right = trade_tile(pk)
    up, down = pk[:PK], pk[3 * PK :]
    filler = jnp.zeros((PK - S - 2, C), BF)
    up = jnp.concatenate(
        [up[:S], from_left[S : S + 1], from_right[S : S + 1], filler], axis=0
    )
    down = jnp.concatenate(
        [down[:S], from_left[S + 1 : S + 2], from_right[S + 1 : S + 2], filler], axis=0
    )
    from_up, from_down = trade_lat(up, down)
    return from_up, from_left, from_right, from_down


def group_ring(kind, step):
    pairs = []
    for t in range(16):
        for l in range(8):
            y, xl, c, xh, z = t // 4, t // 2 % 2, t % 2, l // 4, l % 4
            x = xh * 2 + xl
            if kind == "core":
                c = (c + step) % 2
            elif kind == "z":
                z = (z + step) % 4
            elif kind == "y":
                y = (y + step) % 4
            else:
                x = (x + step) % 4
            to = (y * 4 + x % 2 * 2 + c) * 8 + x // 2 * 4 + z
            pairs.append((t * 8 + l, to))
    return pairs


def move(x, kind, step):
    return lax.ppermute(x, ("tile", "lat"), group_ring(kind, step))


def moves(parts, kind):
    return [move(part, kind, step) for part, step in zip(parts, (1, 3, 2))]


def gathers(part, kind):
    return [move(part, kind, 4 - step) for step in (1, 3, 2)]


def shards(field, cotangent, first_weight, second_weight, side_links, corner_links):
    lat_at = lax.axis_index("lat")
    lon_at = lax.axis_index("tile")
    lk = jnp.concatenate(
        [side_links[lat_at, lon_at].reshape(12), corner_links[lat_at, lon_at].reshape(12)]
    )
    w1 = first_weight.reshape(3, 3 * C, C)
    w2 = second_weight.reshape(3, 3 * C, C)
    cells = field.reshape(CELLS, C)
    cot = cotangent.reshape(CELLS, C)
    cell_bf, cell_f32 = ((CELLS, C), BF), ((CELLS, C), F32)
    edge_bf, edge_f32 = ((4 * S, C), BF), ((4 * S, C), F32)
    halo_bf, turned, packs = ((4 * S, 3 * C), BF), ((C, CELLS), BF), ((4 * PK, C), BF)
    work = 2 * CELLS * 9 * C * C

    far_bf, far_f32 = ((CELLS, C), BF, 1), ((CELLS, C), F32, 1)
    far_turned = ((C, CELLS), BF, 1)

    (pk,) = call(k_pack_field, [field], [packs], links=lk)
    got = trade(pk)
    (cot_e,) = call(k_edges, [cotangent], [edge_bf])
    hidden0, slope0, e0, xt1 = call(
        k_first,
        [cells, w1],
        [far_bf, far_f32, edge_f32, far_turned],
        WIDE,
        after=[got[1]],
        flops=work,
        limit=20,
    )
    halo1, slope_e, hidden_e, pk = call(
        k_first_edges, [*got, e0, w1], [halo_bf, edge_f32, edge_bf, packs], links=lk
    )
    got = trade(pk)
    xt2, mixed0, delta0, e0 = call(
        k_second,
        [hidden_e, hidden0, cot, w2],
        [far_turned, far_bf, far_bf, edge_f32],
        WIDER,
        after=[got[1]],
        flops=work,
        limit=20,
    )
    halo2, mixed_e, delta_e, pk = call(
        k_second_edges, [*got, e0, cot_e, w2], [halo_bf, edge_bf, edge_bf, packs], links=lk
    )
    got = trade(pk)
    total2, fd0, e0 = call(
        k_second_back,
        [delta_e, halo2, delta0, w2, xt2, slope0],
        [far_bf, far_bf, edge_f32],
        WIDER,
        after=[got[1]],
        flops=2 * work,
        limit=22,
    )
    fd_e, pk = call(
        k_first_delta_edges, [*got, e0, slope_e, w1], [edge_bf, packs], links=lk
    )
    core, z_at, y_at = lon_at % 2, lat_at % 4, lon_at // 4
    at = jnp.stack([core, z_at, y_at]).astype(jnp.int32)
    rows_z, rows_y = CELLS // 4, CELLS // 16
    keep, send = call(
        k_first_total,
        [fd_e, halo1, fd0, xt1, total2],
        [cell_bf, cell_bf],
        WIDER + [CELL_BF],
        links=at,
        flops=work,
        limit=20,
    )
    quad_z = [((rows_z, C), F32)] + [((rows_z, C), BF)] * 3
    own, *parts, pk = call(
        k_core_sum, [keep, move(send, "core", 1), pk], quad_z + [packs], links=at
    )
    left, right = trade_tile(pk)
    (middle,) = call(
        k_input_middle, [fd_e, fd0, w1], [cell_f32], WIDER, flops=work, after=[own], limit=18
    )
    quad_y = [((rows_y, C), F32)] + [((rows_y, C), BF)] * 3
    one_pack = ((PK, C), BF)
    own, *parts, up, down = call(
        k_z_sum,
        [own, *moves(parts, "z"), pk, left, right],
        quad_y + [one_pack, one_pack],
        [pltpu.VMEM((rows_z, C), F32)],
        links=at,
        after=[middle],
    )
    up, down = trade_lat(up, down)
    piece_bf = ((rows_y, C), BF)
    (part,) = call(k_y_sum, [own, *moves(parts, "y")], [piece_bf])
    root = math.sqrt(CELLS * lax.axis_size("lat") * lax.axis_size("tile"))
    (part,) = call(
        functools.partial(k_x_sum, 1.0 / root), [part, *moves([part] * 3, "x")], [piece_bf]
    )
    (part,) = call(
        k_join, [part, *gathers(part, "y")], [((rows_z, C), BF)], links=at, after=[up, down]
    )
    parts = [part, *gathers(part, "z")]
    grad, mixed = call(
        k_input_grad,
        [up, left, right, down, middle, mixed0, mixed_e],
        [cell_bf, cell_bf],
        [WIDE[0], WIDER[2]],
        links=lk,
        after=[part],
        limit=16,
    )
    others = [move(part, "core", 1) for part in parts]
    first, second = call(
        k_unpack, [*parts, *others], [cell_f32, cell_f32], links=at, after=[grad], limit=12
    )
    return (
        mixed.reshape(S, S, C),
        grad.reshape(S, S, C),
        first.reshape(3, 3, C, C),
        second.reshape(3, 3, C, C),
    )


def solution(mesh):
    placed = (P("lat", "tile", None), P("lat", "tile", None), P(), P(), P(), P())
    return jax.shard_map(
        shards,
        mesh=mesh,
        in_specs=placed,
        out_specs=(P("lat", "tile", None), P("lat", "tile", None), P(), P()),
        check_vma=False,
    )
```

```python
import functools
import math

import jax
import jax.numpy as jnp
from jax import lax
from jax.experimental import pallas as pl
from jax.experimental.pallas import tpu as pltpu
from jax.sharding import PartitionSpec as P

S = 48
C = 256
CELLS = S * S
ROWS = 8
BLK = ROWS * S
N_BLK = S // ROWS
HALF = 9 * C // 2
PK = 64
F32 = jnp.float32
BF = jnp.bfloat16
MIB = 1 << 20


def side_slot(lk, s):
    return lk[s * 3]


def side_flip(lk, s):
    return lk[s * 3 + 2]


def corner_slot(lk, c):
    return lk[12 + c * 3]


def corner_keep(lk, c):
    return lk[12 + c * 3 + 2]


def side_facing(lk, slot):
    found = jnp.int32(0)
    for s in range(1, 4):
        found = jnp.where(side_slot(lk, s) == slot, jnp.int32(s), found)
    return found


def flip_facing(lk, slot):
    found = side_flip(lk, 0)
    for s in range(1, 4):
        found = jnp.where(side_slot(lk, s) == slot, side_flip(lk, s), found)
    return found


def corner_facing(lk, slot, values):
    found = values[0]
    for c in range(1, 4):
        found = jnp.where(corner_slot(lk, c) == slot, values[c], found)
    return found


def slot_at(lat_step, tile_step):
    return (lat_step + 1) * 3 + tile_step + 1


def package_slots(lk):
    la, ta = lk[24], lk[25]
    return slot_at(la, 0), slot_at(0, ta), slot_at(0, -ta), slot_at(-la, 0)


def package_corners(lk, q):
    la, ta = lk[24], lk[25]
    if q == 1:
        return slot_at(la, ta), slot_at(-la, ta)
    if q == 2:
        return slot_at(la, -ta), slot_at(-la, -ta)
    return ()


def corner_home(lk, c):
    d = corner_slot(lk, c)
    row = jnp.where(d % 3 - 1 == lk[25], jnp.int32(S), jnp.int32(S + 1))
    return row + jnp.where(d // 3 - 1 == lk[24], jnp.int32(0), jnp.int32(3 * PK))


def side_home(lk, s):
    slots = package_slots(lk)
    home = jnp.int32(3 * PK)
    for q in range(3):
        home = jnp.where(side_slot(lk, s) == slots[q], jnp.int32(q * PK), home)
    return home


def grid_of(rows, cols):
    row = lax.broadcasted_iota(jnp.int32, (rows, cols), 0)
    col = lax.broadcasted_iota(jnp.int32, (rows, cols), 1)
    return row, col


def ones_at(hit):
    return jnp.where(hit, 1.0, 0.0).astype(BF)


def pick(hit, rows):
    return jnp.dot(ones_at(hit), rows, preferred_element_type=F32)


def pack_edges(lk, edges):
    row, col = grid_of(PK, 4 * S)
    at = [jnp.int32(c // 2 * S + c % 2 * (S - 1)) for c in range(4)]
    hits = []
    for q, slot in enumerate(package_slots(lk)):
        want = jnp.where(row < S, side_facing(lk, slot) * S + row, -1)
        for k, far in enumerate(package_corners(lk, q)):
            want = jnp.where(row == S + k, corner_facing(lk, far, at), want)
        hits.append(col == want)
    return pick(jnp.concatenate(hits, axis=0), edges).astype(BF)


def pack_rims(lk, rims):
    row, col = grid_of(PK, 4 * PK)
    at = []
    for c in range(4):
        place = jnp.int32(c // 2 * PK + S + c % 2)
        at.append(jnp.where(corner_keep(lk, c) != 0, place, jnp.int32(-1)))
    hits = []
    for q, slot in enumerate(package_slots(lk)):
        cell = jnp.where(flip_facing(lk, slot) == 1, S - 1 - row, row)
        want = jnp.where(row < S, side_facing(lk, slot) * PK + cell, -1)
        for k, far in enumerate(package_corners(lk, q)):
            want = jnp.where(row == S + k, corner_facing(lk, far, at), want)
        hits.append(col == want)
    return pick(jnp.concatenate(hits, axis=0), rims).astype(BF)


def halo_rows(lk, got):
    row, col = grid_of(S, 4 * PK)
    sides = []
    for s in range(4):
        taps = []
        for t in range(3):
            at = row + (t - 1)
            cell = jnp.where(side_flip(lk, s) == 1, S - 1 - at, at)
            want = jnp.where((at >= 0) & (at < S), side_home(lk, s) + cell, -1)
            if s < 2:
                for end, c in ((-1, 2 * s), (S, 2 * s + 1)):
                    home = jnp.where(corner_keep(lk, c) != 0, corner_home(lk, c), -1)
                    want = jnp.where(at == end, home, want)
            taps.append(pick(col == want, got).astype(BF))
        sides.append(jnp.concatenate(taps, axis=1))
    return sides


def rim_adds(lk, got):
    row, col = grid_of(S, 4 * PK)
    adds = []
    for s in range(4):
        hit = col == side_home(lk, s) + row
        if s < 2:
            for end, c in ((0, 2 * s), (S - 1, 2 * s + 1)):
                hit = hit | ((row == end) & (col == corner_home(lk, c)))
        adds.append(pick(hit, got))
    return adds


def cross(adds):
    top, bottom, left, right = adds
    row = lax.broadcasted_iota(jnp.int32, (S, C), 0)
    first = row == 0
    last = row == S - 1

    def with_ends(base, head, tail):
        return base + jnp.where(first, head, 0.0) + jnp.where(last, tail, 0.0)

    return [
        with_ends(top, left[0:1], right[0:1]),
        with_ends(bottom, left[S - 1 :], right[S - 1 :]),
        with_ends(left, top[0:1], bottom[0:1]),
        with_ends(right, top[S - 1 :], bottom[S - 1 :]),
    ]


def gelu_both(z):
    phi = 0.5 + 0.5 * lax.erf(z * (1.0 / math.sqrt(2.0)))
    dens = jnp.exp(z * z * -0.5) * (1.0 / math.sqrt(2.0 * math.pi))
    return z * phi, phi + z * dens


def dot(a, b):
    return jnp.dot(a, b, preferred_element_type=F32)


def dot_nt(a, b):
    return lax.dot_general(a, b, (((1,), (1,)), ((), ())), preferred_element_type=F32)


def halo_sums(sides, w):
    out = [dot(sides[0], w[0]), dot(sides[1], w[2])]
    for s, b in ((2, 0), (3, 2)):
        total = None
        for a in range(3):
            term = dot(sides[s][:, a * C : (a + 1) * C], w[a, b * C : (b + 1) * C])
            total = term if total is None else total + term
        out.append(total)
    return cross(out)


def rims_of(edges, w):
    row, col = grid_of(PK, 4 * S)
    out = []
    for s in range(4):
        total = None
        for t in range(3):
            if s < 2:
                pos = jnp.where(row < S, row + 1, jnp.where(row == S, 0, S + 1))
                used = row < S + 2
                a, b = (0, 2)[s], t
            else:
                pos = row + 1
                used = row < S
                a, b = t, (0, 2)[s - 2]
            src = pos - t
            hit = used & (src >= 0) & (src < S) & (col == s * S + src)
            term = dot_nt(pick(hit, edges).astype(BF), w[a, b * C : (b + 1) * C])
            total = term if total is None else total + term
        out.append(total.astype(BF))
    return jnp.concatenate(out, axis=0)


def put_edges(x, edges):
    x[pl.ds(0, S)] = edges[pl.ds(0, S)]
    x[pl.ds(CELLS - S, S)] = edges[pl.ds(S, S)]
    for r in range(S):
        x[pl.ds(r * S, 1)] = edges[pl.ds(2 * S + r, 1)]
        x[pl.ds(r * S + S - 1, 1)] = edges[pl.ds(3 * S + r, 1)]


def take_edges(x, edges):
    edges[pl.ds(0, S)] = x[pl.ds(0, S)]
    edges[pl.ds(S, S)] = x[pl.ds(CELLS - S, S)]
    for r in range(S):
        edges[pl.ds(2 * S + r, 1)] = x[pl.ds(r * S, 1)]
        edges[pl.ds(3 * S + r, 1)] = x[pl.ds(r * S + S - 1, 1)]


def spread_columns(x, frame, left, right):
    zero = jnp.zeros((S, 3 * C), BF)
    frame[pl.ds(0, S)] = zero
    frame[pl.ds(CELLS + S, S)] = zero
    row = lax.broadcasted_iota(jnp.int32, (S, C), 0)

    @pl.loop(0, S, unroll=4)
    def _(r):
        cells = x[pl.ds(pl.multiple_of(r * S, S), S)]
        to = pl.ds(pl.multiple_of(r * S + S, S), S)
        before = jnp.where(row == 0, 0.0, pltpu.roll(cells, 1, 0))
        after = jnp.where(row == S - 1, 0.0, pltpu.roll(cells, S - 1, 0))
        frame[to, left * C : (left + 1) * C] = before.astype(BF)
        frame[to, C : 2 * C] = cells.astype(BF)
        frame[to, right * C : (right + 1) * C] = after.astype(BF)


def half(i):
    return pl.ds(pl.multiple_of(i * HALF, HALF), HALF)


def block_of(i):
    return pl.ds(i * BLK, BLK)


def conv_block(frame, w, i):
    total = None
    for a in range(3):
        term = dot(frame[pl.ds(i * BLK + a * S, BLK)], w[a])
        total = term if total is None else total + term
    return total


def back_block(frame, w, i):
    total = None
    for a in range(3):
        at = pl.ds(i * BLK + (2 - a) * S, BLK)
        for b in range(3):
            part = frame[at, b * C : (b + 1) * C]
            term = dot_nt(part, w[a, b * C : (b + 1) * C])
            total = term if total is None else total + term
    return total


def weight_sums(xt, frame, halo, edges, store):
    side = []
    for s in range(4):
        side.append(
            lax.dot_general(
                halo[s * S : (s + 1) * S],
                edges[s * S : (s + 1) * S],
                (((0,), (0,)), ((), ())),
                preferred_element_type=F32,
            )
        )
    for a in range(3):
        whole = dot(xt[...], frame[pl.ds((2 - a) * S, CELLS)])
        for b in range(3):
            part = whole[:, b * C : (b + 1) * C]
            if a == 0:
                part = part + side[0][b * C : (b + 1) * C]
            if a == 2:
                part = part + side[1][b * C : (b + 1) * C]
            if b == 0:
                part = part + side[2][a * C : (a + 1) * C]
            if b == 2:
                part = part + side[3][a * C : (a + 1) * C]
            store((a * 3 + b) * C, part.astype(BF))


def column_of(strip, at):
    row = lax.broadcasted_iota(jnp.int32, (S, 16, C), 1)
    return jnp.sum(jnp.where(row == at, strip.astype(F32), 0.0), axis=1).astype(BF)


def edges_of(field):
    right = column_of(field[:, S - 16 :, :], 15)
    return jnp.concatenate(
        [field[0], field[S - 1], column_of(field[:, 0:16, :], 0), right], axis=0
    )


def k_pack_field(at, side, corner, field, pk, links):
    links[24] = 1 - at[3] % 2 * 2
    links[25] = 1 - at[4] % 2 * 2
    for s in range(4):
        for k in range(3):
            links[s * 3 + k] = side[s, k]
            links[12 + s * 3 + k] = corner[s, k]
    pk[...] = pack_edges(links, edges_of(field))


def k_edges(field, after, edges):
    edges[...] = edges_of(field)


def k_second_frame(he, hidden0, frame, xt, x, edges):
    edges[...] = he[...].astype(F32)
    x[...] = hidden0[...].astype(F32)
    put_edges(x, edges)
    xt[...] = x[...].astype(BF).T
    spread_columns(x, frame, 0, 2)


def k_delta_frame(de, delta0, frame, x, edges):
    edges[...] = de[...].astype(F32)
    x[...] = delta0[...].astype(F32)
    put_edges(x, edges)
    spread_columns(x, frame, 2, 0)


def k_first(field, w, after, hidden, slope, e0, xt, x, frame):
    x[...] = field[...].astype(F32)
    xt[...] = field[...].T
    spread_columns(x, frame, 0, 2)

    for i in range(N_BLK):
        to = block_of(i)
        z = conv_block(frame, w, i)
        x[to] = z
        value, grad = gelu_both(z)
        hidden[to] = value.astype(BF)
        slope[to] = grad

    take_edges(x, e0)


def join(got):
    return jnp.concatenate([g[...] for g in got], axis=0)


def k_first_edges(lk, up, left, right, down, e0, w, halo, slope, hidden, pk):
    sides = halo_rows(lk, join((up, left, right, down)))
    for s in range(4):
        halo[pl.ds(s * S, S)] = sides[s]
    z = e0[...] + jnp.concatenate(halo_sums(sides, w), axis=0)
    value, grad = gelu_both(z)
    slope[...] = grad
    hidden[...] = value.astype(BF)
    pk[...] = pack_edges(lk, value.astype(BF))


def k_second(frame, cot, w, after, mixed, delta, e0, x):
    for i in range(N_BLK):
        to = block_of(i)
        z = conv_block(frame, w, i)
        x[to] = z
        value, grad = gelu_both(z)
        mixed[to] = value.astype(BF)
        delta[to] = (cot[to].astype(F32) * grad).astype(BF)

    take_edges(x, e0)


def k_second_edges(lk, up, left, right, down, e0, ec, w, halo, mixed, delta, pk):
    sides = halo_rows(lk, join((up, left, right, down)))
    for s in range(4):
        halo[pl.ds(s * S, S)] = sides[s]
    z = e0[...] + jnp.concatenate(halo_sums(sides, w), axis=0)
    value, grad = gelu_both(z)
    mixed[...] = value.astype(BF)
    edges = (ec[...].astype(F32) * grad).astype(BF)
    delta[...] = edges
    pk[...] = pack_rims(lk, rims_of(edges, w))


def k_second_back(
    at, de, halo, frame, w, xt, slope, after, keep, send, fd, e0, x, tv
):
    for i in range(N_BLK):
        to = block_of(i)
        g = back_block(frame, w, i)
        x[to] = g
        fd[to] = (g * slope[to]).astype(BF)

    take_edges(x, e0)

    def store(row, part):
        tv[pl.ds(row, C)] = part

    weight_sums(xt, frame, halo, de, store)
    keep[...] = tv[half(at[0])]
    send[...] = tv[half(1 - at[0])]


def k_first_delta_edges(lk, up, left, right, down, e0, slope, w, delta, pk):
    adds = cross(rim_adds(lk, join((up, left, right, down))))
    grad = e0[...] + jnp.concatenate(adds, axis=0)
    edges = (grad * slope[...]).astype(BF)
    delta[...] = edges
    pk[...] = pack_rims(lk, rims_of(edges, w))


def k_first_total(at, de, halo, delta0, xt, keep, send, x, frame, edges, tv):
    edges[...] = de[...].astype(F32)
    x[...] = delta0[...].astype(F32)
    put_edges(x, edges)
    spread_columns(x, frame, 2, 0)

    def store(row, part):
        tv[pl.ds(row, C)] = part

    weight_sums(xt, frame, halo, de, store)
    keep[...] = tv[half(at[0])]
    send[...] = tv[half(1 - at[0])]


def k_input_middle(de, delta0, w, after, out, x, frame, edges):
    x[...] = delta0[...].astype(F32)
    edges[...] = de[...].astype(F32)
    put_edges(x, edges)
    spread_columns(x, frame, 2, 0)

    for i in range(N_BLK):
        out[block_of(i)] = back_block(frame, w, i)


def k_input_grad(lk, up, left, right, down, middle, mixed0, me, after, out, mixed, token, x, edges):
    adds = cross(rim_adds(lk, join((up, left, right, down))))
    x[...] = middle[...]
    take_edges(x, edges)
    edges[...] += jnp.concatenate(adds, axis=0)
    put_edges(x, edges)
    out[...] = x[...].astype(BF)
    x[...] = mixed0[...].astype(F32)
    edges[...] = me[...].astype(F32)
    put_edges(x, edges)
    mixed[...] = x[...].astype(BF)
    token[...] = jnp.zeros_like(token)


STEPS = (0, 1, 3, 2)


def quarter(place, step, rows):
    return pl.ds(pl.multiple_of((place ^ step) * rows, 16), rows)


def k_core_sum(at, keep1, got1, keep2, got2, pk, own, s1, s3, s2, pk_out):
    rows = own.shape[0] // 2
    for step, out in zip(STEPS, (own, s1, s3, s2)):
        part = quarter(at[1], step, rows)
        for k, (keep, got) in enumerate(((keep1, got1), (keep2, got2))):
            total = keep[part].astype(F32) + got[part].astype(F32)
            out[pl.ds(k * rows, rows)] = total.astype(out.dtype)
    pk_out[...] = pk[...]


def k_z_sum(at, own, g1, g3, g2, pk, left, right, after, o, s1, s3, s2, up_out, down_out, x):
    rows = o.shape[0]
    x[...] = (own[...] + g2[...].astype(F32)) + (g1[...].astype(F32) + g3[...].astype(F32))
    for step, out in zip(STEPS, (o, s1, s3, s2)):
        out[...] = x[quarter(at[2], step, rows)].astype(out.dtype)
    up_out[...] = with_corners(pk[0:PK], left[...], right[...], 0)
    down_out[...] = with_corners(pk[3 * PK :], left[...], right[...], 1)


def with_corners(edge, left, right, k):
    row = lax.broadcasted_iota(jnp.int32, (PK, C), 0)
    out = jnp.where(row == S, left[S + k : S + k + 1].astype(F32), edge.astype(F32))
    return jnp.where(row == S + 1, right[S + k : S + k + 1].astype(F32), out).astype(BF)


def k_y_sum(own, g1, g3, g2, up, down, out):
    total = (own[...] + g2[...].astype(F32)) + (g1[...].astype(F32) + g3[...].astype(F32))
    out[...] = total.astype(BF)


def k_x_sum(scale, own, g1, g3, g2, out):
    total = (own[...].astype(F32) + g2[...].astype(F32)) + (
        g1[...].astype(F32) + g3[...].astype(F32)
    )
    out[...] = (total * scale).astype(BF)


def k_join(at, own, g1, g3, g2, after, out):
    rows = own.shape[0]
    for step, part in zip(STEPS, (own, g1, g3, g2)):
        out[quarter(at[2], step, rows)] = part[...]


def unpack(core, at, parts, first, second, buf, sems):
    rows = HALF // 4
    copies = []
    for q, (step, part) in enumerate(zip(STEPS, parts)):
        place = core * HALF + (at[1] ^ step) * rows
        to = pl.ds(pl.multiple_of(place, 16), rows)
        buf[q] = part[...].astype(F32)
        for k, out in enumerate((first, second)):
            copy = pltpu.make_async_copy(
                buf.at[q, pl.ds(k * rows, rows)], out.at[to], sems.at[2 * q + k]
            )
            copy.start()
            copies.append(copy)
    for copy in copies:
        copy.wait()


def k_unpack_own(at, a0, a1, a3, a2, after, first, second, buf, sems):
    unpack(at[0], at, (a0, a1, a3, a2), first, second, buf, sems)


def k_unpack_other(at, b0, b1, b3, b2, first_in, second_in, first, second, buf, sems):
    unpack(1 - at[0], at, (b0, b1, b3, b2), first, second, buf, sems)


VMEM = pl.BlockSpec(memory_space=pltpu.VMEM)
SMEM = pl.BlockSpec(memory_space=pltpu.SMEM)
ANY = pl.BlockSpec(memory_space=pl.ANY)
HBM = pl.BlockSpec(memory_space=pltpu.HBM)
CELL_BF = pltpu.VMEM((CELLS, C), BF)
WIDE = [pltpu.VMEM((CELLS, C), F32), pltpu.VMEM((CELLS + 2 * S, 3 * C), BF)]
WIDER = WIDE + [pltpu.VMEM((4 * S, C), F32)]


def call(kernel, args, outs, scratch=(), links=None, flops=0, after=(), limit=8, hbm=(), alias=None, out_specs=None):
    given = ([links] if links is not None else []) + [*args, *hbm, *after]
    specs = ([SMEM] if links is not None else []) + [VMEM] * len(args)
    specs += [HBM] * len(hbm) + [ANY] * len(after)
    name = getattr(kernel, "__name__", None) or kernel.func.__name__
    return pl.pallas_call(
        kernel,
        out_shape=[
            (pltpu.VMEM if len(out) > 2 else jax.ShapeDtypeStruct)(out[0], out[1]) for out in outs
        ],
        in_specs=specs,
        out_specs=out_specs or [VMEM] * len(outs),
        input_output_aliases=alias or {},
        scratch_shapes=list(scratch),
        compiler_params=pltpu.CompilerParams(vmem_limit_bytes=limit * MIB),
        cost_estimate=pl.CostEstimate(
            flops=int(flops), bytes_accessed=4 * MIB, transcendentals=0
        ),
        name=name,
    )(*given)


def pairs_a(count):
    return [(i, i ^ 1) for i in range(count)]


def pairs_b(count):
    return [(i, (i + 1 if i % 2 else i - 1) % count) for i in range(count)]


def trade_tile(pk):
    n = lax.axis_size("tile")
    from_a = lax.ppermute(pk[PK : 2 * PK], "tile", pairs_a(n))
    from_b = lax.ppermute(pk[2 * PK : 3 * PK], "tile", pairs_b(n))
    return from_a, from_b


def trade_lat(to_a, to_b):
    n = lax.axis_size("lat")
    return lax.ppermute(to_a, "lat", pairs_a(n)), lax.ppermute(to_b, "lat", pairs_b(n))


def trade(pk):
    tile_a, tile_b = trade_tile(pk)
    filler = jnp.zeros((PK - S - 2, C), BF)

    def with_cells(edge, k):
        cells = [tile_a[S + k : S + k + 1], tile_b[S + k : S + k + 1]]
        return jnp.concatenate([edge[:S], *cells, filler], axis=0)

    lat_a, lat_b = trade_lat(with_cells(pk[:PK], 0), with_cells(pk[3 * PK :], 1))
    return lat_a, tile_a, tile_b, lat_b


def exchange(kind, step):
    pairs = []
    for t in range(16):
        for l in range(8):
            y, xl, c, xh, z = t // 4, t // 2 % 2, t % 2, l // 4, l % 4
            x = xh * 2 + xl
            if kind == "core":
                c ^= step
            elif kind == "z":
                z ^= step
            elif kind == "y":
                y ^= step
            else:
                x ^= step
            to = (y * 4 + x % 2 * 2 + c) * 8 + x // 2 * 4 + z
            pairs.append((t * 8 + l, to))
    return pairs


def move(x, kind, step):
    return lax.ppermute(x, ("tile", "lat"), exchange(kind, step))


def moves(parts, kind):
    return [move(part, kind, step) for part, step in zip(parts, STEPS[1:])]


def gathers(part, kind):
    return [move(part, kind, step) for step in STEPS[1:]]


def shards(field, cotangent, first_weight, second_weight, side_links, corner_links):
    lat_at = lax.axis_index("lat")
    lon_at = lax.axis_index("tile")
    core, z_at, y_at = lon_at % 2, lat_at % 4, lon_at // 4
    at = jnp.stack([core, z_at, y_at, lat_at, lon_at]).astype(jnp.int32)
    w1 = first_weight.reshape(3, 3 * C, C)
    w2 = second_weight.reshape(3, 3 * C, C)
    cells = field.reshape(CELLS, C)
    cot = cotangent.reshape(CELLS, C)
    cell_bf, cell_f32 = ((CELLS, C), BF), ((CELLS, C), F32)
    edge_bf, edge_f32 = ((4 * S, C), BF), ((4 * S, C), F32)
    halo_bf, turned, packs = ((4 * S, 3 * C), BF), ((C, CELLS), BF), ((4 * PK, C), BF)
    work = 2 * CELLS * 9 * C * C

    far_bf, far_f32 = ((CELLS, C), BF, 1), ((CELLS, C), F32, 1)
    far_turned = ((C, CELLS), BF, 1)

    frame_bf = ((CELLS + 2 * S, 3 * C), BF, 1)
    half_bf = ((HALF, C), BF)

    own_side = side_links[lat_at, lon_at]
    own_corner = corner_links[lat_at, lon_at]
    pk, lk = pl.pallas_call(
        k_pack_field,
        out_shape=[jax.ShapeDtypeStruct(*packs), jax.ShapeDtypeStruct((26,), jnp.int32)],
        in_specs=[SMEM, SMEM, SMEM, VMEM],
        out_specs=[VMEM, SMEM],
        compiler_params=pltpu.CompilerParams(vmem_limit_bytes=8 * MIB),
        name="k_pack_field",
    )(at, own_side, own_corner, field)
    got = trade(pk)
    (cot_e,) = call(k_edges, [cotangent], [edge_bf], after=[got[1]])
    hidden0, slope0, e0, xt1 = call(
        k_first,
        [cells, w1],
        [far_bf, far_f32, edge_f32, far_turned],
        WIDE,
        after=[got[1]],
        flops=work,
        limit=18,
    )
    halo1, slope_e, hidden_e, pk = call(
        k_first_edges, [*got, e0, w1], [halo_bf, edge_f32, edge_bf, packs], links=lk
    )
    got = trade(pk)
    frame, xt2 = call(
        k_second_frame, [hidden_e, hidden0], [frame_bf, far_turned], [WIDE[0], WIDER[2]], limit=14
    )
    mixed0, delta0, e0 = call(
        k_second,
        [frame, cot, w2],
        [far_bf, far_bf, edge_f32],
        WIDE[:1],
        after=[got[1]],
        flops=work,
        limit=18,
    )
    halo2, mixed_e, delta_e, pk = call(
        k_second_edges, [*got, e0, cot_e, w2], [halo_bf, edge_bf, edge_bf, packs], links=lk
    )
    got = trade(pk)
    (frame,) = call(
        k_delta_frame, [delta_e, delta0], [frame_bf], [WIDE[0], WIDER[2]], limit=12
    )
    keep2, send2, fd0, e0 = call(
        k_second_back,
        [delta_e, halo2, frame, w2, xt2, slope0],
        [half_bf, half_bf, far_bf, edge_f32],
        [WIDE[0], CELL_BF],
        links=at,
        after=[got[1]],
        flops=2 * work,
        limit=22,
    )
    got2 = move(send2, "core", 1)
    fd_e, pk = call(
        k_first_delta_edges, [*got, e0, slope_e, w1], [edge_bf, packs], links=lk
    )
    keep1, send1 = call(
        k_first_total,
        [fd_e, halo1, fd0, xt1],
        [half_bf, half_bf],
        WIDER + [CELL_BF],
        links=at,
        flops=work,
        limit=20,
    )
    got1 = move(send1, "core", 1)
    rows_z, rows_y = CELLS // 4, CELLS // 16
    quad_z = [((rows_z, C), F32)] + [((rows_z, C), BF)] * 3
    own, *parts, pk = call(
        k_core_sum, [keep1, got1, keep2, got2, pk], quad_z + [packs], links=at
    )
    left, right = trade_tile(pk)
    (middle,) = call(
        k_input_middle, [fd_e, fd0, w1], [cell_f32], WIDER, flops=work, after=[own], limit=18
    )
    quad_y = [((rows_y, C), F32)] + [((rows_y, C), BF)] * 3
    one_pack = ((PK, C), BF)
    own, *parts, up, down = call(
        k_z_sum,
        [own, *moves(parts, "z"), pk, left, right],
        quad_y + [one_pack, one_pack],
        [pltpu.VMEM((rows_z, C), F32)],
        links=at,
        after=[middle],
    )
    up, down = trade_lat(up, down)
    piece_bf = ((rows_y, C), BF)
    (part,) = call(k_y_sum, [own, *moves(parts, "y")], [piece_bf], after=[up, down])
    grad, mixed, token = call(
        k_input_grad,
        [up, left, right, down, middle, mixed0, mixed_e],
        [cell_bf, cell_bf, ((8, 128), F32)],
        [WIDE[0], WIDER[2]],
        links=lk,
        after=[part],
        limit=16,
    )
    root = math.sqrt(CELLS * lax.axis_size("lat") * lax.axis_size("tile"))
    (part,) = call(
        functools.partial(k_x_sum, 1.0 / root), [part, *moves([part] * 3, "x")], [piece_bf]
    )
    (part,) = call(
        k_join, [part, *gathers(part, "y")], [((rows_z, C), BF)], links=at, after=[token]
    )
    parts = [part, *gathers(part, "z")]
    others = [move(part, "core", 1) for part in parts]
    buffers = [pltpu.VMEM((4, rows_z, C), F32), pltpu.SemaphoreType.DMA((8,))]
    sums = call(
        k_unpack_own, parts, [cell_f32, cell_f32], buffers, links=at, out_specs=[HBM, HBM],
        after=[parts[0]],
    )
    first, second = call(
        k_unpack_other,
        others,
        [cell_f32, cell_f32],
        buffers,
        links=at,
        hbm=sums,
        alias={5: 0, 6: 1},
        out_specs=[HBM, HBM],
    )
    return (
        mixed.reshape(S, S, C),
        grad.reshape(S, S, C),
        first.reshape(3, 3, C, C),
        second.reshape(3, 3, C, C),
    )


def solution(mesh):
    placed = (P("lat", "tile", None), P("lat", "tile", None), P(), P(), P(), P())
    return jax.shard_map(
        shards,
        mesh=mesh,
        in_specs=placed,
        out_specs=(P("lat", "tile", None), P("lat", "tile", None), P(), P()),
        check_vma=False,
    )
```

```python
import functools
import math

import jax
import jax.numpy as jnp
from jax import lax
from jax.experimental import pallas as pl
from jax.experimental.pallas import tpu as pltpu
from jax.sharding import PartitionSpec as P

S = 48
C = 256
CELLS = S * S
ROWS = 8
BLK = ROWS * S
N_BLK = S // ROWS
HALF = 9 * C // 2
PK = 64
F32 = jnp.float32
BF = jnp.bfloat16
MIB = 1 << 20


def side_slot(lk, s):
    return lk[s * 3]


def side_flip(lk, s):
    return lk[s * 3 + 2]


def corner_slot(lk, c):
    return lk[12 + c * 3]


def corner_keep(lk, c):
    return lk[12 + c * 3 + 2]


def side_facing(lk, slot):
    found = jnp.int32(0)
    for s in range(1, 4):
        found = jnp.where(side_slot(lk, s) == slot, jnp.int32(s), found)
    return found


def flip_facing(lk, slot):
    found = side_flip(lk, 0)
    for s in range(1, 4):
        found = jnp.where(side_slot(lk, s) == slot, side_flip(lk, s), found)
    return found


def corner_facing(lk, slot, values):
    found = values[0]
    for c in range(1, 4):
        found = jnp.where(corner_slot(lk, c) == slot, values[c], found)
    return found


def slot_at(lat_step, tile_step):
    return (lat_step + 1) * 3 + tile_step + 1


def package_slots(lk):
    la, ta = lk[24], lk[25]
    return slot_at(la, 0), slot_at(0, ta), slot_at(0, -ta), slot_at(-la, 0)


def package_corners(lk, q):
    la, ta = lk[24], lk[25]
    if q == 1:
        return slot_at(la, ta), slot_at(-la, ta)
    if q == 2:
        return slot_at(la, -ta), slot_at(-la, -ta)
    return ()


def corner_home(lk, c):
    d = corner_slot(lk, c)
    row = jnp.where(d % 3 - 1 == lk[25], jnp.int32(S), jnp.int32(S + 1))
    return row + jnp.where(d // 3 - 1 == lk[24], jnp.int32(0), jnp.int32(3 * PK))


def side_home(lk, s):
    slots = package_slots(lk)
    home = jnp.int32(3 * PK)
    for q in range(3):
        home = jnp.where(side_slot(lk, s) == slots[q], jnp.int32(q * PK), home)
    return home


def grid_of(rows, cols):
    row = lax.broadcasted_iota(jnp.int32, (rows, cols), 0)
    col = lax.broadcasted_iota(jnp.int32, (rows, cols), 1)
    return row, col


def ones_at(hit):
    return jnp.where(hit, 1.0, 0.0).astype(BF)


def pick(hit, rows):
    return jnp.dot(ones_at(hit), rows, preferred_element_type=F32)


def pack_edges(lk, edges):
    row, col = grid_of(PK, 4 * S)
    at = [jnp.int32(c // 2 * S + c % 2 * (S - 1)) for c in range(4)]
    hits = []
    for q, slot in enumerate(package_slots(lk)):
        want = jnp.where(row < S, side_facing(lk, slot) * S + row, -1)
        for k, far in enumerate(package_corners(lk, q)):
            want = jnp.where(row == S + k, corner_facing(lk, far, at), want)
        hits.append(col == want)
    return pick(jnp.concatenate(hits, axis=0), edges).astype(BF)


def pack_rims(lk, rims):
    row, col = grid_of(PK, 4 * PK)
    at = []
    for c in range(4):
        place = jnp.int32(c // 2 * PK + S + c % 2)
        at.append(jnp.where(corner_keep(lk, c) != 0, place, jnp.int32(-1)))
    hits = []
    for q, slot in enumerate(package_slots(lk)):
        cell = jnp.where(flip_facing(lk, slot) == 1, S - 1 - row, row)
        want = jnp.where(row < S, side_facing(lk, slot) * PK + cell, -1)
        for k, far in enumerate(package_corners(lk, q)):
            want = jnp.where(row == S + k, corner_facing(lk, far, at), want)
        hits.append(col == want)
    return pick(jnp.concatenate(hits, axis=0), rims).astype(BF)


def halo_rows(lk, got):
    row, col = grid_of(S, 4 * PK)
    sides = []
    for s in range(4):
        taps = []
        for t in range(3):
            at = row + (t - 1)
            cell = jnp.where(side_flip(lk, s) == 1, S - 1 - at, at)
            want = jnp.where((at >= 0) & (at < S), side_home(lk, s) + cell, -1)
            if s < 2:
                for end, c in ((-1, 2 * s), (S, 2 * s + 1)):
                    home = jnp.where(corner_keep(lk, c) != 0, corner_home(lk, c), -1)
                    want = jnp.where(at == end, home, want)
            taps.append(pick(col == want, got).astype(BF))
        sides.append(jnp.concatenate(taps, axis=1))
    return sides


def rim_adds(lk, got):
    row, col = grid_of(S, 4 * PK)
    adds = []
    for s in range(4):
        hit = col == side_home(lk, s) + row
        if s < 2:
            for end, c in ((0, 2 * s), (S - 1, 2 * s + 1)):
                hit = hit | ((row == end) & (col == corner_home(lk, c)))
        adds.append(pick(hit, got))
    return adds


def cross(adds):
    top, bottom, left, right = adds
    row = lax.broadcasted_iota(jnp.int32, (S, C), 0)
    first = row == 0
    last = row == S - 1

    def with_ends(base, head, tail):
        return base + jnp.where(first, head, 0.0) + jnp.where(last, tail, 0.0)

    return [
        with_ends(top, left[0:1], right[0:1]),
        with_ends(bottom, left[S - 1 :], right[S - 1 :]),
        with_ends(left, top[0:1], bottom[0:1]),
        with_ends(right, top[S - 1 :], bottom[S - 1 :]),
    ]


def gelu_both(z):
    phi = 0.5 + 0.5 * lax.erf(z * (1.0 / math.sqrt(2.0)))
    dens = jnp.exp(z * z * -0.5) * (1.0 / math.sqrt(2.0 * math.pi))
    return z * phi, phi + z * dens


def dot(a, b):
    return jnp.dot(a, b, preferred_element_type=F32)


def dot_nt(a, b):
    return lax.dot_general(a, b, (((1,), (1,)), ((), ())), preferred_element_type=F32)


def halo_sums(sides, w):
    out = [dot(sides[0], w[0]), dot(sides[1], w[2])]
    for s, b in ((2, 0), (3, 2)):
        total = None
        for a in range(3):
            term = dot(sides[s][:, a * C : (a + 1) * C], w[a, b * C : (b + 1) * C])
            total = term if total is None else total + term
        out.append(total)
    return cross(out)


def rims_of(edges, w):
    row, col = grid_of(PK, 4 * S)
    out = []
    for s in range(4):
        total = None
        for t in range(3):
            if s < 2:
                pos = jnp.where(row < S, row + 1, jnp.where(row == S, 0, S + 1))
                used = row < S + 2
                a, b = (0, 2)[s], t
            else:
                pos = row + 1
                used = row < S
                a, b = t, (0, 2)[s - 2]
            src = pos - t
            hit = used & (src >= 0) & (src < S) & (col == s * S + src)
            term = dot_nt(pick(hit, edges).astype(BF), w[a, b * C : (b + 1) * C])
            total = term if total is None else total + term
        out.append(total.astype(BF))
    return jnp.concatenate(out, axis=0)


def put_edges(x, edges):
    x[pl.ds(0, S)] = edges[pl.ds(0, S)]
    x[pl.ds(CELLS - S, S)] = edges[pl.ds(S, S)]
    for r in range(S):
        x[pl.ds(r * S, 1)] = edges[pl.ds(2 * S + r, 1)]
        x[pl.ds(r * S + S - 1, 1)] = edges[pl.ds(3 * S + r, 1)]


def take_edges(x, edges):
    edges[pl.ds(0, S)] = x[pl.ds(0, S)]
    edges[pl.ds(S, S)] = x[pl.ds(CELLS - S, S)]
    for r in range(S):
        edges[pl.ds(2 * S + r, 1)] = x[pl.ds(r * S, 1)]
        edges[pl.ds(3 * S + r, 1)] = x[pl.ds(r * S + S - 1, 1)]


def spread_columns(x, frame, left, right):
    zero = jnp.zeros((S, 3 * C), BF)
    frame[pl.ds(0, S)] = zero
    frame[pl.ds(CELLS + S, S)] = zero
    row = lax.broadcasted_iota(jnp.int32, (S, C), 0)

    @pl.loop(0, S, unroll=4)
    def _(r):
        cells = x[pl.ds(pl.multiple_of(r * S, S), S)]
        to = pl.ds(pl.multiple_of(r * S + S, S), S)
        before = jnp.where(row == 0, 0.0, pltpu.roll(cells, 1, 0))
        after = jnp.where(row == S - 1, 0.0, pltpu.roll(cells, S - 1, 0))
        frame[to, left * C : (left + 1) * C] = before.astype(BF)
        frame[to, C : 2 * C] = cells.astype(BF)
        frame[to, right * C : (right + 1) * C] = after.astype(BF)


def half(i):
    return pl.ds(pl.multiple_of(i * HALF, HALF), HALF)


def block_of(i):
    return pl.ds(i * BLK, BLK)


def conv_block(frame, w, i):
    total = None
    for a in range(3):
        term = dot(frame[pl.ds(i * BLK + a * S, BLK)], w[a])
        total = term if total is None else total + term
    return total


def back_block(frame, w, i):
    total = None
    for a in range(3):
        at = pl.ds(i * BLK + (2 - a) * S, BLK)
        for b in range(3):
            part = frame[at, b * C : (b + 1) * C]
            term = dot_nt(part, w[a, b * C : (b + 1) * C])
            total = term if total is None else total + term
    return total


def weight_sums(xt, frame, halo, edges, store):
    side = []
    for s in range(4):
        side.append(
            lax.dot_general(
                halo[s * S : (s + 1) * S],
                edges[s * S : (s + 1) * S],
                (((0,), (0,)), ((), ())),
                preferred_element_type=F32,
            )
        )
    for a in range(3):
        whole = dot(xt[...], frame[pl.ds((2 - a) * S, CELLS)])
        for b in range(3):
            part = whole[:, b * C : (b + 1) * C]
            if a == 0:
                part = part + side[0][b * C : (b + 1) * C]
            if a == 2:
                part = part + side[1][b * C : (b + 1) * C]
            if b == 0:
                part = part + side[2][a * C : (a + 1) * C]
            if b == 2:
                part = part + side[3][a * C : (a + 1) * C]
            store((a * 3 + b) * C, part.astype(BF))


def column_of(strip, at):
    row = lax.broadcasted_iota(jnp.int32, (S, 16, C), 1)
    return jnp.sum(jnp.where(row == at, strip.astype(F32), 0.0), axis=1).astype(BF)


def edges_of(field):
    right = column_of(field[:, S - 16 :, :], 15)
    return jnp.concatenate(
        [field[0], field[S - 1], column_of(field[:, 0:16, :], 0), right], axis=0
    )


def k_pack_field(at, side, corner, field, pk, links, cells):
    cells[...] = field[...].reshape(CELLS, C)
    links[24] = 1 - at[3] % 2 * 2
    links[25] = 1 - at[4] % 2 * 2
    for s in range(4):
        for k in range(3):
            links[s * 3 + k] = side[s, k]
            links[12 + s * 3 + k] = corner[s, k]
    pk[...] = pack_edges(links, edges_of(field))


def k_edges(field, after, edges):
    edges[...] = edges_of(field)


def k_second_frame(he, hidden0, frame, xt, x, edges):
    edges[...] = he[...].astype(F32)
    x[...] = hidden0[...].astype(F32)
    put_edges(x, edges)
    xt[...] = x[...].astype(BF).T
    spread_columns(x, frame, 0, 2)


def k_delta_frame(de, delta0, frame, x, edges):
    edges[...] = de[...].astype(F32)
    x[...] = delta0[...].astype(F32)
    put_edges(x, edges)
    spread_columns(x, frame, 2, 0)


def k_first_frame(field, frame, xt, x):
    x[...] = field[...].astype(F32)
    xt[...] = field[...].T
    spread_columns(x, frame, 0, 2)


def k_first(frame, w, after, hidden, slope, e0, x):
    for i in range(N_BLK):
        to = block_of(i)
        z = conv_block(frame, w, i)
        x[to] = z
        value, grad = gelu_both(z)
        hidden[to] = value.astype(BF)
        slope[to] = grad

    take_edges(x, e0)


def join(got):
    return jnp.concatenate([g[...] for g in got], axis=0)


def k_first_edges(lk, up, left, right, down, e0, w, halo, slope, hidden, pk):
    sides = halo_rows(lk, join((up, left, right, down)))
    for s in range(4):
        halo[pl.ds(s * S, S)] = sides[s]
    z = e0[...] + jnp.concatenate(halo_sums(sides, w), axis=0)
    value, grad = gelu_both(z)
    slope[...] = grad
    hidden[...] = value.astype(BF)
    pk[...] = pack_edges(lk, value.astype(BF))


def k_second(frame, cot, w, after, mixed, delta, e0, x):
    for i in range(N_BLK):
        to = block_of(i)
        z = conv_block(frame, w, i)
        x[to] = z
        value, grad = gelu_both(z)
        mixed[to] = value.astype(BF)
        delta[to] = (cot[to].astype(F32) * grad).astype(BF)

    take_edges(x, e0)


def k_second_edges(lk, up, left, right, down, e0, ec, w, halo, mixed, delta, pk):
    sides = halo_rows(lk, join((up, left, right, down)))
    for s in range(4):
        halo[pl.ds(s * S, S)] = sides[s]
    z = e0[...] + jnp.concatenate(halo_sums(sides, w), axis=0)
    value, grad = gelu_both(z)
    mixed[...] = value.astype(BF)
    edges = (ec[...].astype(F32) * grad).astype(BF)
    delta[...] = edges
    pk[...] = pack_rims(lk, rims_of(edges, w))


def k_second_back(
    at, de, halo, frame, w, xt, slope, after, keep, send, fd, e0, x, tv
):
    for i in range(N_BLK):
        to = block_of(i)
        g = back_block(frame, w, i)
        x[to] = g
        fd[to] = (g * slope[to]).astype(BF)

    take_edges(x, e0)

    def store(row, part):
        tv[pl.ds(row, C)] = part

    weight_sums(xt, frame, halo, de, store)
    keep[...] = tv[half(at[0])]
    send[...] = tv[half(1 - at[0])]


def k_first_delta_edges(lk, up, left, right, down, e0, slope, w, delta, pk):
    adds = cross(rim_adds(lk, join((up, left, right, down))))
    grad = e0[...] + jnp.concatenate(adds, axis=0)
    edges = (grad * slope[...]).astype(BF)
    delta[...] = edges
    pk[...] = pack_rims(lk, rims_of(edges, w))


def k_first_total(at, de, halo, delta0, xt, keep, send, x, frame, edges, tv):
    edges[...] = de[...].astype(F32)
    x[...] = delta0[...].astype(F32)
    put_edges(x, edges)
    spread_columns(x, frame, 2, 0)

    def store(row, part):
        tv[pl.ds(row, C)] = part

    weight_sums(xt, frame, halo, de, store)
    keep[...] = tv[half(at[0])]
    send[...] = tv[half(1 - at[0])]


def k_input_middle(de, delta0, w, after, out, x, frame, edges):
    x[...] = delta0[...].astype(F32)
    edges[...] = de[...].astype(F32)
    put_edges(x, edges)
    spread_columns(x, frame, 2, 0)

    for i in range(N_BLK):
        out[block_of(i)] = back_block(frame, w, i)


def k_input_grad(lk, up, left, right, down, middle, mixed0, me, after, out, mixed, token, x, edges):
    adds = cross(rim_adds(lk, join((up, left, right, down))))
    x[...] = middle[...]
    take_edges(x, edges)
    edges[...] += jnp.concatenate(adds, axis=0)
    put_edges(x, edges)
    out[...] = x[...].astype(BF)
    x[...] = mixed0[...].astype(F32)
    edges[...] = me[...].astype(F32)
    put_edges(x, edges)
    mixed[...] = x[...].astype(BF)
    token[...] = jnp.zeros_like(token)


STEPS = (0, 1, 3, 2)


def quarter(place, step, rows):
    return pl.ds(pl.multiple_of((place ^ step) * rows, 16), rows)


def k_core_sum(at, keep1, got1, keep2, got2, pk, own, s1, s3, s2, pk_out):
    rows = own.shape[0] // 2
    for step, out in zip(STEPS, (own, s1, s3, s2)):
        part = quarter(at[1], step, rows)
        for k, (keep, got) in enumerate(((keep1, got1), (keep2, got2))):
            total = keep[part].astype(F32) + got[part].astype(F32)
            out[pl.ds(k * rows, rows)] = total.astype(out.dtype)
    pk_out[...] = pk[...]


def k_z_sum(at, own, g2, g3, g1, *refs):
    o, s1, s3, s2, x = refs[-5:]
    rows = o.shape[0]
    x[...] = (own[...] + g2[...].astype(F32)) + (g1[...].astype(F32) + g3[...].astype(F32))
    for step, out in zip(STEPS, (o, s1, s3, s2)):
        out[...] = x[quarter(at[2], step, rows)].astype(out.dtype)


def k_y_sum(own, g1, g3, g2, out):
    total = (own[...] + g2[...].astype(F32)) + (g1[...].astype(F32) + g3[...].astype(F32))
    out[...] = total.astype(BF)


def k_x_sum(scale, own, g1, g3, g2, out):
    total = (own[...].astype(F32) + g2[...].astype(F32)) + (
        g1[...].astype(F32) + g3[...].astype(F32)
    )
    out[...] = (total * scale).astype(BF)


def k_join(at, own, g1, g3, g2, after, out):
    rows = own.shape[0]
    for step, part in zip(STEPS, (own, g1, g3, g2)):
        out[quarter(at[2], step, rows)] = part[...]


def unpack(core, at, parts, first, second, buf, sems):
    rows = HALF // 4
    copies = []
    for q, (step, part) in enumerate(zip(STEPS, parts)):
        place = core * HALF + (at[1] ^ step) * rows
        to = pl.ds(pl.multiple_of(place, 16), rows)
        buf[q] = part[...].astype(F32)
        for k, out in enumerate((first, second)):
            copy = pltpu.make_async_copy(
                buf.at[q, pl.ds(k * rows, rows)], out.at[to], sems.at[2 * q + k]
            )
            copy.start()
            copies.append(copy)
    for copy in copies:
        copy.wait()


def k_unpack_own(at, a0, a1, a3, a2, after, first, second, buf, sems):
    unpack(at[0], at, (a0, a1, a3, a2), first, second, buf, sems)


def k_unpack_other(at, b0, b1, b3, b2, first_in, second_in, first, second, buf, sems):
    unpack(1 - at[0], at, (b0, b1, b3, b2), first, second, buf, sems)


VMEM = pl.BlockSpec(memory_space=pltpu.VMEM)
SMEM = pl.BlockSpec(memory_space=pltpu.SMEM)
ANY = pl.BlockSpec(memory_space=pl.ANY)
HBM = pl.BlockSpec(memory_space=pltpu.HBM)
CELL_BF = pltpu.VMEM((CELLS, C), BF)
WIDE = [pltpu.VMEM((CELLS, C), F32), pltpu.VMEM((CELLS + 2 * S, 3 * C), BF)]
WIDER = WIDE + [pltpu.VMEM((4 * S, C), F32)]


def call(kernel, args, outs, scratch=(), links=None, flops=0, after=(), limit=8, hbm=(), alias=None, out_specs=None):
    given = ([links] if links is not None else []) + [*args, *hbm, *after]
    specs = ([SMEM] if links is not None else []) + [VMEM] * len(args)
    specs += [HBM] * len(hbm) + [ANY] * len(after)
    name = getattr(kernel, "__name__", None) or kernel.func.__name__
    return pl.pallas_call(
        kernel,
        out_shape=[
            (pltpu.VMEM if len(out) > 2 else jax.ShapeDtypeStruct)(out[0], out[1]) for out in outs
        ],
        in_specs=specs,
        out_specs=out_specs or [VMEM] * len(outs),
        input_output_aliases=alias or {},
        scratch_shapes=list(scratch),
        compiler_params=pltpu.CompilerParams(vmem_limit_bytes=limit * MIB),
        cost_estimate=pl.CostEstimate(
            flops=int(flops), bytes_accessed=4 * MIB, transcendentals=0
        ),
        name=name,
    )(*given)


def pairs_a(count):
    return [(i, i ^ 1) for i in range(count)]


def pairs_b(count):
    return [(i, (i + 1 if i % 2 else i - 1) % count) for i in range(count)]


def trade_tile(pk):
    n = lax.axis_size("tile")
    from_a = lax.ppermute(pk[PK : 2 * PK], "tile", pairs_a(n))
    from_b = lax.ppermute(pk[2 * PK : 3 * PK], "tile", pairs_b(n))
    return from_a, from_b


def trade_lat(to_a, to_b):
    n = lax.axis_size("lat")
    return lax.ppermute(to_a, "lat", pairs_a(n)), lax.ppermute(to_b, "lat", pairs_b(n))


def trade(pk):
    tile_a, tile_b = trade_tile(pk)
    filler = jnp.zeros((PK - S - 2, C), BF)

    def with_cells(edge, k):
        cells = [tile_a[S + k : S + k + 1], tile_b[S + k : S + k + 1]]
        return jnp.concatenate([edge[:S], *cells, filler], axis=0)

    lat_a, lat_b = trade_lat(with_cells(pk[:PK], 0), with_cells(pk[3 * PK :], 1))
    return lat_a, tile_a, tile_b, lat_b


def exchange(kind, step):
    pairs = []
    for t in range(16):
        for l in range(8):
            y, xl, c, xh, z = t // 4, t // 2 % 2, t % 2, l // 4, l % 4
            x = xh * 2 + xl
            if kind == "core":
                c ^= step
            elif kind == "z":
                z ^= step
            elif kind == "y":
                y ^= step
            else:
                x ^= step
            to = (y * 4 + x % 2 * 2 + c) * 8 + x // 2 * 4 + z
            pairs.append((t * 8 + l, to))
    return pairs


def move(x, kind, step):
    return lax.ppermute(x, ("tile", "lat"), exchange(kind, step))


def moves(parts, kind):
    return [move(part, kind, step) for part, step in zip(parts, STEPS[1:])]


def gathers(part, kind):
    return [move(part, kind, step) for step in STEPS[1:]]


def shards(field, cotangent, first_weight, second_weight, side_links, corner_links):
    lat_at = lax.axis_index("lat")
    lon_at = lax.axis_index("tile")
    core, z_at, y_at = lon_at % 2, lat_at % 4, lon_at // 4
    at = jnp.stack([core, z_at, y_at, lat_at, lon_at]).astype(jnp.int32)
    w1 = first_weight.reshape(3, 3 * C, C)
    w2 = second_weight.reshape(3, 3 * C, C)
    cot = cotangent.reshape(CELLS, C)
    cell_bf, cell_f32 = ((CELLS, C), BF), ((CELLS, C), F32)
    edge_bf, edge_f32 = ((4 * S, C), BF), ((4 * S, C), F32)
    halo_bf, turned, packs = ((4 * S, 3 * C), BF), ((C, CELLS), BF), ((4 * PK, C), BF)
    work = 2 * CELLS * 9 * C * C

    far_bf, far_f32 = ((CELLS, C), BF, 1), ((CELLS, C), F32, 1)
    far_turned = ((C, CELLS), BF, 1)

    frame_bf = ((CELLS + 2 * S, 3 * C), BF, 1)
    half_bf = ((HALF, C), BF)

    own_side = side_links[lat_at, lon_at]
    own_corner = corner_links[lat_at, lon_at]
    pk, lk, cells = pl.pallas_call(
        k_pack_field,
        out_shape=[jax.ShapeDtypeStruct(*packs), jax.ShapeDtypeStruct((26,), jnp.int32), pltpu.VMEM((CELLS, C), BF)],
        in_specs=[SMEM, SMEM, SMEM, VMEM],
        out_specs=[VMEM, SMEM, VMEM],
        compiler_params=pltpu.CompilerParams(vmem_limit_bytes=8 * MIB),
        name="k_pack_field",
    )(at, own_side, own_corner, field)
    got = trade(pk)
    frame, xt1 = call(k_first_frame, [cells], [frame_bf, far_turned], WIDE[:1], limit=12)
    (cot_e,) = call(k_edges, [cotangent], [edge_bf], after=[got[1]])
    hidden0, slope0, e0 = call(
        k_first,
        [frame, w1],
        [far_bf, far_f32, edge_f32],
        WIDE[:1],
        after=[got[1]],
        flops=work,
        limit=18,
    )
    halo1, slope_e, hidden_e, pk = call(
        k_first_edges, [*got, e0, w1], [halo_bf, edge_f32, edge_bf, packs], links=lk
    )
    got = trade(pk)
    frame, xt2 = call(
        k_second_frame, [hidden_e, hidden0], [frame_bf, far_turned], [WIDE[0], WIDER[2]], limit=14
    )
    mixed0, delta0, e0 = call(
        k_second,
        [frame, cot, w2],
        [far_bf, far_bf, edge_f32],
        WIDE[:1],
        after=[got[1]],
        flops=work,
        limit=18,
    )
    halo2, mixed_e, delta_e, pk = call(
        k_second_edges, [*got, e0, cot_e, w2], [halo_bf, edge_bf, edge_bf, packs], links=lk
    )
    got = trade(pk)
    (frame,) = call(
        k_delta_frame, [delta_e, delta0], [frame_bf], [WIDE[0], WIDER[2]], limit=12
    )
    keep2, send2, fd0, e0 = call(
        k_second_back,
        [delta_e, halo2, frame, w2, xt2, slope0],
        [half_bf, half_bf, far_bf, edge_f32],
        [WIDE[0], CELL_BF],
        links=at,
        after=[got[1]],
        flops=2 * work,
        limit=22,
    )
    got2 = move(send2, "core", 1)
    fd_e, pk = call(
        k_first_delta_edges, [*got, e0, slope_e, w1], [edge_bf, packs], links=lk
    )
    keep1, send1 = call(
        k_first_total,
        [fd_e, halo1, fd0, xt1],
        [half_bf, half_bf],
        WIDER + [CELL_BF],
        links=at,
        flops=work,
        limit=20,
    )
    got1 = move(send1, "core", 1)
    rows_z, rows_y = CELLS // 4, CELLS // 16
    quad_z = [((rows_z, C), F32)] + [((rows_z, C), BF)] * 3
    own, *parts, pk = call(
        k_core_sum, [keep1, got1, keep2, got2, pk], quad_z + [packs], links=at
    )
    got = trade(pk)
    (middle,) = call(
        k_input_middle, [fd_e, fd0, w1], [cell_f32], WIDER, flops=work, after=[got[1]], limit=18
    )
    quad_y = [((rows_y, C), F32)] + [((rows_y, C), BF)] * 3
    own, *parts = call(
        k_z_sum,
        [own, *moves(parts, "z")[::-1]],
        quad_y,
        [pltpu.VMEM((rows_z, C), F32)],
        links=at,
        after=[middle, got[0], got[3]],
    )
    piece_bf = ((rows_y, C), BF)
    (part,) = call(k_y_sum, [own, *moves(parts, "y")], [piece_bf])
    grad, mixed, token = call(
        k_input_grad,
        [*got, middle, mixed0, mixed_e],
        [cell_bf, cell_bf, ((8, 128), F32)],
        [WIDE[0], WIDER[2]],
        links=lk,
        after=[part],
        limit=16,
    )
    root = math.sqrt(CELLS * lax.axis_size("lat") * lax.axis_size("tile"))
    (part,) = call(
        functools.partial(k_x_sum, 1.0 / root), [part, *moves([part] * 3, "x")], [piece_bf]
    )
    (part,) = call(
        k_join, [part, *gathers(part, "y")], [((rows_z, C), BF)], links=at, after=[token]
    )
    parts = [part, *gathers(part, "z")]
    others = [move(part, "core", 1) for part in parts]
    buffers = [pltpu.VMEM((4, rows_z, C), F32), pltpu.SemaphoreType.DMA((8,))]
    sums = call(
        k_unpack_own, parts, [cell_f32, cell_f32], buffers, links=at, out_specs=[HBM, HBM],
        after=[parts[0]],
    )
    first, second = call(
        k_unpack_other,
        others,
        [cell_f32, cell_f32],
        buffers,
        links=at,
        hbm=sums,
        alias={5: 0, 6: 1},
        out_specs=[HBM, HBM],
    )
    return (
        mixed.reshape(S, S, C),
        grad.reshape(S, S, C),
        first.reshape(3, 3, C, C),
        second.reshape(3, 3, C, C),
    )


def solution(mesh):
    placed = (P("lat", "tile", None), P("lat", "tile", None), P(), P(), P(), P())
    return jax.shard_map(
        shards,
        mesh=mesh,
        in_specs=placed,
        out_specs=(P("lat", "tile", None), P("lat", "tile", None), P(), P()),
        check_vma=False,
    )
```

```python
import functools
import math

import jax
import jax.numpy as jnp
from jax import lax
from jax.experimental import pallas as pl
from jax.experimental.pallas import tpu as pltpu
from jax.sharding import PartitionSpec as P

S = 48
C = 256
CELLS = S * S
ROWS = 8
BLK = ROWS * S
N_BLK = S // ROWS
HALF = 9 * C // 2
PK = 64
F32 = jnp.float32
BF = jnp.bfloat16
MIB = 1 << 20


def side_slot(lk, s):
    return lk[s * 3]


def side_flip(lk, s):
    return lk[s * 3 + 2]


def corner_slot(lk, c):
    return lk[12 + c * 3]


def corner_keep(lk, c):
    return lk[12 + c * 3 + 2]


def side_facing(lk, slot):
    found = jnp.int32(0)
    for s in range(1, 4):
        found = jnp.where(side_slot(lk, s) == slot, jnp.int32(s), found)
    return found


def flip_facing(lk, slot):
    found = side_flip(lk, 0)
    for s in range(1, 4):
        found = jnp.where(side_slot(lk, s) == slot, side_flip(lk, s), found)
    return found


def corner_facing(lk, slot, values):
    found = values[0]
    for c in range(1, 4):
        found = jnp.where(corner_slot(lk, c) == slot, values[c], found)
    return found


def slot_at(lat_step, tile_step):
    return (lat_step + 1) * 3 + tile_step + 1


def package_slots(lk):
    la, ta = lk[24], lk[25]
    return slot_at(la, 0), slot_at(0, ta), slot_at(0, -ta), slot_at(-la, 0)


def package_corners(lk, q):
    la, ta = lk[24], lk[25]
    if q == 1:
        return slot_at(la, ta), slot_at(-la, ta)
    if q == 2:
        return slot_at(la, -ta), slot_at(-la, -ta)
    return ()


def corner_home(lk, c):
    d = corner_slot(lk, c)
    row = jnp.where(d % 3 - 1 == lk[25], jnp.int32(S), jnp.int32(S + 1))
    return row + jnp.where(d // 3 - 1 == lk[24], jnp.int32(0), jnp.int32(3 * PK))


def side_home(lk, s):
    slots = package_slots(lk)
    home = jnp.int32(3 * PK)
    for q in range(3):
        home = jnp.where(side_slot(lk, s) == slots[q], jnp.int32(q * PK), home)
    return home


def grid_of(rows, cols):
    row = lax.broadcasted_iota(jnp.int32, (rows, cols), 0)
    col = lax.broadcasted_iota(jnp.int32, (rows, cols), 1)
    return row, col


def ones_at(hit):
    return jnp.where(hit, 1.0, 0.0).astype(BF)


def pick(hit, rows):
    return jnp.dot(ones_at(hit), rows, preferred_element_type=F32)


def pack_edges(lk, edges):
    row, col = grid_of(PK, 4 * S)
    at = [jnp.int32(c // 2 * S + c % 2 * (S - 1)) for c in range(4)]
    hits = []
    for q, slot in enumerate(package_slots(lk)):
        want = jnp.where(row < S, side_facing(lk, slot) * S + row, -1)
        for k, far in enumerate(package_corners(lk, q)):
            want = jnp.where(row == S + k, corner_facing(lk, far, at), want)
        hits.append(col == want)
    return pick(jnp.concatenate(hits, axis=0), edges).astype(BF)


def pack_rims(lk, rims):
    row, col = grid_of(PK, 4 * PK)
    at = []
    for c in range(4):
        place = jnp.int32(c // 2 * PK + S + c % 2)
        at.append(jnp.where(corner_keep(lk, c) != 0, place, jnp.int32(-1)))
    hits = []
    for q, slot in enumerate(package_slots(lk)):
        cell = jnp.where(flip_facing(lk, slot) == 1, S - 1 - row, row)
        want = jnp.where(row < S, side_facing(lk, slot) * PK + cell, -1)
        for k, far in enumerate(package_corners(lk, q)):
            want = jnp.where(row == S + k, corner_facing(lk, far, at), want)
        hits.append(col == want)
    return pick(jnp.concatenate(hits, axis=0), rims).astype(BF)


def halo_rows(lk, got):
    row, col = grid_of(S, 4 * PK)
    hits = []
    for s in range(4):
        for t in range(3):
            at = row + (t - 1)
            cell = jnp.where(side_flip(lk, s) == 1, S - 1 - at, at)
            want = jnp.where((at >= 0) & (at < S), side_home(lk, s) + cell, -1)
            if s < 2:
                for end, c in ((-1, 2 * s), (S, 2 * s + 1)):
                    home = jnp.where(corner_keep(lk, c) != 0, corner_home(lk, c), -1)
                    want = jnp.where(at == end, home, want)
            hits.append(col == want)
    cells = pick(jnp.concatenate(hits, axis=0), got).astype(BF)
    taps = [cells[n * S : (n + 1) * S] for n in range(12)]
    return [jnp.concatenate(taps[3 * s : 3 * s + 3], axis=1) for s in range(4)]


def rim_adds(lk, got):
    row, col = grid_of(S, 4 * PK)
    hits = []
    for s in range(4):
        hit = col == side_home(lk, s) + row
        if s < 2:
            for end, c in ((0, 2 * s), (S - 1, 2 * s + 1)):
                hit = hit | ((row == end) & (col == corner_home(lk, c)))
        hits.append(hit)
    adds = pick(jnp.concatenate(hits, axis=0), got)
    return [adds[s * S : (s + 1) * S] for s in range(4)]


def cross(adds):
    top, bottom, left, right = adds
    row = lax.broadcasted_iota(jnp.int32, (S, C), 0)
    first = row == 0
    last = row == S - 1

    def with_ends(base, head, tail):
        return base + jnp.where(first, head, 0.0) + jnp.where(last, tail, 0.0)

    return [
        with_ends(top, left[0:1], right[0:1]),
        with_ends(bottom, left[S - 1 :], right[S - 1 :]),
        with_ends(left, top[0:1], bottom[0:1]),
        with_ends(right, top[S - 1 :], bottom[S - 1 :]),
    ]


def gelu_both(z):
    phi = 0.5 + 0.5 * lax.erf(z * (1.0 / math.sqrt(2.0)))
    dens = jnp.exp(z * z * -0.5) * (1.0 / math.sqrt(2.0 * math.pi))
    return z * phi, phi + z * dens


def dot(a, b):
    return jnp.dot(a, b, preferred_element_type=F32)


def dot_nt(a, b):
    return lax.dot_general(a, b, (((1,), (1,)), ((), ())), preferred_element_type=F32)


def halo_sums(sides, w):
    out = [dot(sides[0], w[0]), dot(sides[1], w[2])]
    for s, b in ((2, 0), (3, 2)):
        total = None
        for a in range(3):
            term = dot(sides[s][:, a * C : (a + 1) * C], w[a, b * C : (b + 1) * C])
            total = term if total is None else total + term
        out.append(total)
    return cross(out)


def rims_of(edges, w):
    row, col = grid_of(PK, 4 * S)
    hits = []
    for s in range(4):
        for t in range(3):
            if s < 2:
                pos = jnp.where(row < S, row + 1, jnp.where(row == S, 0, S + 1))
                used = row < S + 2
            else:
                pos = row + 1
                used = row < S
            src = pos - t
            hits.append(used & (src >= 0) & (src < S) & (col == s * S + src))
    cells = pick(jnp.concatenate(hits, axis=0), edges).astype(BF)
    out = []
    for s in range(4):
        total = None
        for t in range(3):
            a, b = ((0, 2)[s], t) if s < 2 else (t, (0, 2)[s - 2])
            n = 3 * s + t
            term = dot_nt(cells[n * PK : (n + 1) * PK], w[a, b * C : (b + 1) * C])
            total = term if total is None else total + term
        out.append(total.astype(BF))
    return jnp.concatenate(out, axis=0)


def put_edges(x, edges):
    x[pl.ds(0, S)] = edges[pl.ds(0, S)]
    x[pl.ds(CELLS - S, S)] = edges[pl.ds(S, S)]
    for r in range(S):
        x[pl.ds(r * S, 1)] = edges[pl.ds(2 * S + r, 1)]
        x[pl.ds(r * S + S - 1, 1)] = edges[pl.ds(3 * S + r, 1)]


def take_edges(x, edges):
    edges[pl.ds(0, S)] = x[pl.ds(0, S)]
    edges[pl.ds(S, S)] = x[pl.ds(CELLS - S, S)]
    for r in range(S):
        edges[pl.ds(2 * S + r, 1)] = x[pl.ds(r * S, 1)]
        edges[pl.ds(3 * S + r, 1)] = x[pl.ds(r * S + S - 1, 1)]


def spread_columns(x, frame, left, right):
    zero = jnp.zeros((S, 3 * C), BF)
    frame[pl.ds(0, S)] = zero
    frame[pl.ds(CELLS + S, S)] = zero
    row = lax.broadcasted_iota(jnp.int32, (S, C), 0)

    @pl.loop(0, S, unroll=4)
    def _(r):
        cells = x[pl.ds(pl.multiple_of(r * S, S), S)]
        to = pl.ds(pl.multiple_of(r * S + S, S), S)
        before = jnp.where(row == 0, 0.0, pltpu.roll(cells, 1, 0))
        after = jnp.where(row == S - 1, 0.0, pltpu.roll(cells, S - 1, 0))
        frame[to, left * C : (left + 1) * C] = before.astype(BF)
        frame[to, C : 2 * C] = cells.astype(BF)
        frame[to, right * C : (right + 1) * C] = after.astype(BF)


def half(i):
    return pl.ds(pl.multiple_of(i * HALF, HALF), HALF)


def block_of(i):
    return pl.ds(i * BLK, BLK)


def conv_block(frame, w, i):
    total = None
    for a in range(3):
        term = dot(frame[pl.ds(i * BLK + a * S, BLK)], w[a])
        total = term if total is None else total + term
    return total


def back_block(frame, w, i):
    total = None
    for a in range(3):
        at = pl.ds(i * BLK + (2 - a) * S, BLK)
        for b in range(3):
            part = frame[at, b * C : (b + 1) * C]
            term = dot_nt(part, w[a, b * C : (b + 1) * C])
            total = term if total is None else total + term
    return total


def weight_sums(xt, frame, halo, edges, store):
    side = []
    for s in range(4):
        side.append(
            lax.dot_general(
                halo[s * S : (s + 1) * S],
                edges[s * S : (s + 1) * S],
                (((0,), (0,)), ((), ())),
                preferred_element_type=F32,
            )
        )
    for a in range(3):
        whole = dot(xt[...], frame[pl.ds((2 - a) * S, CELLS)])
        for b in range(3):
            part = whole[:, b * C : (b + 1) * C]
            if a == 0:
                part = part + side[0][b * C : (b + 1) * C]
            if a == 2:
                part = part + side[1][b * C : (b + 1) * C]
            if b == 0:
                part = part + side[2][a * C : (a + 1) * C]
            if b == 2:
                part = part + side[3][a * C : (a + 1) * C]
            store((a * 3 + b) * C, part.astype(BF))


def column_of(strip, at):
    row = lax.broadcasted_iota(jnp.int32, (S, 16, C), 1)
    return jnp.sum(jnp.where(row == at, strip.astype(F32), 0.0), axis=1).astype(BF)


def edges_of(field):
    right = column_of(field[:, S - 16 :, :], 15)
    return jnp.concatenate(
        [field[0], field[S - 1], column_of(field[:, 0:16, :], 0), right], axis=0
    )


def k_pack_field(at, side, corner, field, pk, links, cells):
    cells[...] = field[...].reshape(CELLS, C)
    links[24] = 1 - at[3] % 2 * 2
    links[25] = 1 - at[4] % 2 * 2
    for s in range(4):
        for k in range(3):
            links[s * 3 + k] = side[s, k]
            links[12 + s * 3 + k] = corner[s, k]
    pk[...] = pack_edges(links, edges_of(field))


def k_edges(field, after, edges):
    edges[...] = edges_of(field)


def k_second_frame(he, hidden0, frame, xt, x, edges):
    edges[...] = he[...].astype(F32)
    x[...] = hidden0[...].astype(F32)
    put_edges(x, edges)
    xt[...] = x[...].astype(BF).T
    spread_columns(x, frame, 0, 2)


def k_delta_frame(de, delta0, frame, x, edges):
    edges[...] = de[...].astype(F32)
    x[...] = delta0[...].astype(F32)
    put_edges(x, edges)
    spread_columns(x, frame, 2, 0)


def k_first_frame(field, frame, xt, x):
    x[...] = field[...].astype(F32)
    xt[...] = field[...].T
    spread_columns(x, frame, 0, 2)


def k_first(frame, w, after, hidden, slope, e0, x):
    for i in range(N_BLK):
        to = block_of(i)
        z = conv_block(frame, w, i)
        x[to] = z
        value, grad = gelu_both(z)
        hidden[to] = value.astype(BF)
        slope[to] = grad

    take_edges(x, e0)


def join(got):
    return jnp.concatenate([g[...] for g in got], axis=0)


def k_first_edges(lk, up, left, right, down, e0, w, halo, slope, hidden, pk):
    sides = halo_rows(lk, join((up, left, right, down)))
    for s in range(4):
        halo[pl.ds(s * S, S)] = sides[s]
    z = e0[...] + jnp.concatenate(halo_sums(sides, w), axis=0)
    value, grad = gelu_both(z)
    slope[...] = grad
    hidden[...] = value.astype(BF)
    pk[...] = pack_edges(lk, value.astype(BF))


def k_second(frame, cot, w, after, mixed, delta, e0, x):
    for i in range(N_BLK):
        to = block_of(i)
        z = conv_block(frame, w, i)
        x[to] = z
        value, grad = gelu_both(z)
        mixed[to] = value.astype(BF)
        delta[to] = (cot[to].astype(F32) * grad).astype(BF)

    take_edges(x, e0)


def k_second_edges(lk, up, left, right, down, e0, ec, w, halo, mixed, delta, pk):
    sides = halo_rows(lk, join((up, left, right, down)))
    for s in range(4):
        halo[pl.ds(s * S, S)] = sides[s]
    z = e0[...] + jnp.concatenate(halo_sums(sides, w), axis=0)
    value, grad = gelu_both(z)
    mixed[...] = value.astype(BF)
    edges = (ec[...].astype(F32) * grad).astype(BF)
    delta[...] = edges
    pk[...] = pack_rims(lk, rims_of(edges, w))


def k_second_back(
    at, de, halo, frame, w, xt, slope, after, keep, send, fd, e0, x, tv
):
    for i in range(N_BLK):
        to = block_of(i)
        g = back_block(frame, w, i)
        x[to] = g
        fd[to] = (g * slope[to]).astype(BF)

    take_edges(x, e0)

    def store(row, part):
        tv[pl.ds(row, C)] = part

    weight_sums(xt, frame, halo, de, store)
    keep[...] = tv[half(at[0])]
    send[...] = tv[half(1 - at[0])]


def k_first_delta_edges(lk, up, left, right, down, e0, slope, w, delta, pk):
    adds = cross(rim_adds(lk, join((up, left, right, down))))
    grad = e0[...] + jnp.concatenate(adds, axis=0)
    edges = (grad * slope[...]).astype(BF)
    delta[...] = edges
    pk[...] = pack_rims(lk, rims_of(edges, w))


def half_sums(h, xt, frame, side, out):
    for n in range(4):
        tap = h * 5 + n
        a, b = tap // 3, tap % 3
        rows = pl.ds(pl.multiple_of((2 - a) * S, 16), CELLS)
        lanes = pl.ds(pl.multiple_of(b * C, C), C)
        part = dot(xt[...], frame[rows, lanes])
        for k, (used, at) in enumerate(((a == 0, b), (a == 2, b), (b == 0, a), (b == 2, a))):
            term = side[pl.ds(pl.multiple_of(k * 3 * C + at * C, C), C)]
            part = part + jnp.where(used, term, 0.0)
        out[pl.ds(pl.multiple_of(n * C + h * (C // 2), C // 2), C)] = part.astype(BF)
    part = dot(xt[pl.ds(pl.multiple_of(h * (C // 2), C // 2), C // 2)], frame[pl.ds(S, CELLS), C : 2 * C])
    out[pl.ds(pl.multiple_of((1 - h) * 4 * C, C), C // 2)] = part.astype(BF)


def k_first_send(at, de, halo, delta0, xt, send, frame, side, x, edges):
    edges[...] = de[...].astype(F32)
    x[...] = delta0[...].astype(F32)
    put_edges(x, edges)
    spread_columns(x, frame, 2, 0)
    for s in range(4):
        side[pl.ds(s * 3 * C, 3 * C)] = lax.dot_general(
            halo[s * S : (s + 1) * S],
            de[s * S : (s + 1) * S],
            (((0,), (0,)), ((), ())),
            preferred_element_type=F32,
        )
    half_sums(1 - at[0], xt, frame, side, send)


def k_first_keep(at, xt, frame, side, keep):
    half_sums(at[0], xt, frame, side, keep)


def k_input_middle(de, delta0, w, after, out, x, frame, edges):
    x[...] = delta0[...].astype(F32)
    edges[...] = de[...].astype(F32)
    put_edges(x, edges)
    spread_columns(x, frame, 2, 0)

    for i in range(N_BLK):
        out[block_of(i)] = back_block(frame, w, i)


def k_input_grad(lk, up, left, right, down, middle, mixed0, me, after, out, mixed, token, x, edges):
    adds = cross(rim_adds(lk, join((up, left, right, down))))
    x[...] = middle[...]
    take_edges(x, edges)
    edges[...] += jnp.concatenate(adds, axis=0)
    put_edges(x, edges)
    out[...] = x[...].astype(BF)
    x[...] = mixed0[...].astype(F32)
    edges[...] = me[...].astype(F32)
    put_edges(x, edges)
    mixed[...] = x[...].astype(BF)
    token[...] = jnp.zeros_like(token)


STEPS = (0, 1, 3, 2)


def quarter(place, step, rows):
    return pl.ds(pl.multiple_of((place ^ step) * rows, 16), rows)


def k_core_sum(at, keep1, got1, keep2, got2, pk, own, s1, s3, s2, pk_out):
    rows = own.shape[0] // 2
    for step, out in zip(STEPS, (own, s1, s3, s2)):
        part = quarter(at[1], step, rows)
        for k, (keep, got) in enumerate(((keep1, got1), (keep2, got2))):
            total = keep[part].astype(F32) + got[part].astype(F32)
            out[pl.ds(k * rows, rows)] = total.astype(out.dtype)
    pk_out[...] = pk[...]


def k_z_sum(at, own, g2, g3, g1, *refs):
    o, s1, s3, s2, x = refs[-5:]
    rows = o.shape[0]
    x[...] = (own[...] + g2[...].astype(F32)) + (g1[...].astype(F32) + g3[...].astype(F32))
    for step, out in zip(STEPS, (o, s1, s3, s2)):
        out[...] = x[quarter(at[2], step, rows)].astype(out.dtype)


def k_y_sum(own, g1, g3, g2, out):
    total = (own[...] + g2[...].astype(F32)) + (g1[...].astype(F32) + g3[...].astype(F32))
    out[...] = total.astype(BF)


def k_x_sum(scale, own, g1, g3, g2, out):
    total = (own[...].astype(F32) + g2[...].astype(F32)) + (
        g1[...].astype(F32) + g3[...].astype(F32)
    )
    out[...] = (total * scale).astype(BF)


def k_join(at, own, g1, g3, g2, after, out):
    rows = own.shape[0]
    for step, part in zip(STEPS, (own, g1, g3, g2)):
        out[quarter(at[2], step, rows)] = part[...]


def unpack(core, at, parts, first, second, buf, sems):
    rows = HALF // 4
    copies = []
    for q, (step, part) in enumerate(zip(STEPS, parts)):
        place = core * HALF + (at[1] ^ step) * rows
        to = pl.ds(pl.multiple_of(place, 16), rows)
        buf[q] = part[...].astype(F32)
        for k, out in enumerate((first, second)):
            copy = pltpu.make_async_copy(
                buf.at[q, pl.ds(k * rows, rows)], out.at[to], sems.at[2 * q + k]
            )
            copy.start()
            copies.append(copy)
    for copy in copies:
        copy.wait()


def k_unpack_own(at, a0, a1, a3, a2, after, first, second, buf, sems):
    unpack(at[0], at, (a0, a1, a3, a2), first, second, buf, sems)


def k_unpack_other(at, b0, b1, b3, b2, first_in, second_in, first, second, buf, sems):
    unpack(1 - at[0], at, (b0, b1, b3, b2), first, second, buf, sems)


VMEM = pl.BlockSpec(memory_space=pltpu.VMEM)
SMEM = pl.BlockSpec(memory_space=pltpu.SMEM)
ANY = pl.BlockSpec(memory_space=pl.ANY)
HBM = pl.BlockSpec(memory_space=pltpu.HBM)
CELL_BF = pltpu.VMEM((CELLS, C), BF)
WIDE = [pltpu.VMEM((CELLS, C), F32), pltpu.VMEM((CELLS + 2 * S, 3 * C), BF)]
WIDER = WIDE + [pltpu.VMEM((4 * S, C), F32)]


def call(kernel, args, outs, scratch=(), links=None, flops=0, after=(), limit=8, hbm=(), alias=None, out_specs=None):
    given = ([links] if links is not None else []) + [*args, *hbm, *after]
    specs = ([SMEM] if links is not None else []) + [VMEM] * len(args)
    specs += [HBM] * len(hbm) + [ANY] * len(after)
    name = getattr(kernel, "__name__", None) or kernel.func.__name__
    return pl.pallas_call(
        kernel,
        out_shape=[
            (pltpu.VMEM if len(out) > 2 else jax.ShapeDtypeStruct)(out[0], out[1]) for out in outs
        ],
        in_specs=specs,
        out_specs=out_specs or [VMEM] * len(outs),
        input_output_aliases=alias or {},
        scratch_shapes=list(scratch),
        compiler_params=pltpu.CompilerParams(vmem_limit_bytes=limit * MIB),
        cost_estimate=pl.CostEstimate(
            flops=int(flops), bytes_accessed=4 * MIB, transcendentals=0
        ),
        name=name,
    )(*given)


def pairs_a(count):
    return [(i, i ^ 1) for i in range(count)]


def pairs_b(count):
    return [(i, (i + 1 if i % 2 else i - 1) % count) for i in range(count)]


def trade_tile(pk):
    n = lax.axis_size("tile")
    from_a = lax.ppermute(pk[PK : 2 * PK], "tile", pairs_a(n))
    from_b = lax.ppermute(pk[2 * PK : 3 * PK], "tile", pairs_b(n))
    return from_a, from_b


def trade_lat(to_a, to_b):
    n = lax.axis_size("lat")
    return lax.ppermute(to_a, "lat", pairs_a(n)), lax.ppermute(to_b, "lat", pairs_b(n))


def trade(pk):
    tile_a, tile_b = trade_tile(pk)
    filler = jnp.zeros((PK - S - 2, C), BF)

    def with_cells(edge, k):
        cells = [tile_a[S + k : S + k + 1], tile_b[S + k : S + k + 1]]
        return jnp.concatenate([edge[:S], *cells, filler], axis=0)

    lat_a, lat_b = trade_lat(with_cells(pk[:PK], 0), with_cells(pk[3 * PK :], 1))
    return lat_a, tile_a, tile_b, lat_b


def exchange(kind, step):
    pairs = []
    for t in range(16):
        for l in range(8):
            y, xl, c, xh, z = t // 4, t // 2 % 2, t % 2, l // 4, l % 4
            x = xh * 2 + xl
            if kind == "core":
                c ^= step
            elif kind == "z":
                z ^= step
            elif kind == "y":
                y ^= step
            else:
                x ^= step
            to = (y * 4 + x % 2 * 2 + c) * 8 + x // 2 * 4 + z
            pairs.append((t * 8 + l, to))
    return pairs


def move(x, kind, step):
    return lax.ppermute(x, ("tile", "lat"), exchange(kind, step))


def moves(parts, kind):
    return [move(part, kind, step) for part, step in zip(parts, STEPS[1:])]


def gathers(part, kind):
    return [move(part, kind, step) for step in STEPS[1:]]


def shards(field, cotangent, first_weight, second_weight, side_links, corner_links):
    lat_at = lax.axis_index("lat")
    lon_at = lax.axis_index("tile")
    core, z_at, y_at = lon_at % 2, lat_at % 4, lon_at // 4
    at = jnp.stack([core, z_at, y_at, lat_at, lon_at]).astype(jnp.int32)
    w1 = first_weight.reshape(3, 3 * C, C)
    w2 = second_weight.reshape(3, 3 * C, C)
    cot = cotangent.reshape(CELLS, C)
    cell_bf, cell_f32 = ((CELLS, C), BF), ((CELLS, C), F32)
    edge_bf, edge_f32 = ((4 * S, C), BF), ((4 * S, C), F32)
    halo_bf, turned, packs = ((4 * S, 3 * C), BF), ((C, CELLS), BF), ((4 * PK, C), BF)
    work = 2 * CELLS * 9 * C * C

    far_bf, far_f32 = ((CELLS, C), BF, 1), ((CELLS, C), F32, 1)
    far_turned = ((C, CELLS), BF, 1)

    frame_bf = ((CELLS + 2 * S, 3 * C), BF, 1)
    half_bf = ((HALF, C), BF)

    own_side = side_links[lat_at, lon_at]
    own_corner = corner_links[lat_at, lon_at]
    pk, lk, cells = pl.pallas_call(
        k_pack_field,
        out_shape=[jax.ShapeDtypeStruct(*packs), jax.ShapeDtypeStruct((26,), jnp.int32), pltpu.VMEM((CELLS, C), BF)],
        in_specs=[SMEM, SMEM, SMEM, VMEM],
        out_specs=[VMEM, SMEM, VMEM],
        compiler_params=pltpu.CompilerParams(vmem_limit_bytes=8 * MIB),
        name="k_pack_field",
    )(at, own_side, own_corner, field)
    got = trade(pk)
    frame, xt1 = call(k_first_frame, [cells], [frame_bf, far_turned], WIDE[:1], limit=12)
    (cot_e,) = call(k_edges, [cotangent], [edge_bf], after=[got[1]])
    hidden0, slope0, e0 = call(
        k_first,
        [frame, w1],
        [far_bf, far_f32, edge_f32],
        WIDE[:1],
        after=[got[1]],
        flops=work,
        limit=18,
    )
    halo1, slope_e, hidden_e, pk = call(
        k_first_edges, [*got, e0, w1], [halo_bf, edge_f32, edge_bf, packs], links=lk
    )
    got = trade(pk)
    frame, xt2 = call(
        k_second_frame, [hidden_e, hidden0], [frame_bf, far_turned], [WIDE[0], WIDER[2]], limit=14
    )
    mixed0, delta0, e0 = call(
        k_second,
        [frame, cot, w2],
        [far_bf, far_bf, edge_f32],
        WIDE[:1],
        after=[got[1]],
        flops=work,
        limit=18,
    )
    halo2, mixed_e, delta_e, pk = call(
        k_second_edges, [*got, e0, cot_e, w2], [halo_bf, edge_bf, edge_bf, packs], links=lk
    )
    got = trade(pk)
    (frame,) = call(
        k_delta_frame, [delta_e, delta0], [frame_bf], [WIDE[0], WIDER[2]], limit=12
    )
    keep2, send2, fd0, e0 = call(
        k_second_back,
        [delta_e, halo2, frame, w2, xt2, slope0],
        [half_bf, half_bf, far_bf, edge_f32],
        [WIDE[0], CELL_BF],
        links=at,
        after=[got[1]],
        flops=2 * work,
        limit=22,
    )
    got2 = move(send2, "core", 1)
    fd_e, pk = call(
        k_first_delta_edges, [*got, e0, slope_e, w1], [edge_bf, packs], links=lk
    )
    send1, frame, side = call(
        k_first_send,
        [fd_e, halo1, fd0, xt1],
        [half_bf, frame_bf, ((12 * C, C), F32, 1)],
        [WIDE[0], WIDER[2]],
        links=at,
        flops=work,
        limit=20,
    )
    got1 = move(send1, "core", 1)
    (keep1,) = call(
        k_first_keep, [xt1, frame, side], [half_bf], links=at, flops=work, limit=14
    )
    rows_z, rows_y = CELLS // 4, CELLS // 16
    quad_z = [((rows_z, C), F32)] + [((rows_z, C), BF)] * 3
    own, *parts, pk = call(
        k_core_sum, [keep1, got1, keep2, got2, pk], quad_z + [packs], links=at
    )
    got = trade(pk)
    (middle,) = call(
        k_input_middle, [fd_e, fd0, w1], [cell_f32], WIDER, flops=work, after=[got[1]], limit=18
    )
    quad_y = [((rows_y, C), F32)] + [((rows_y, C), BF)] * 3
    own, *parts = call(
        k_z_sum,
        [own, *moves(parts, "z")[::-1]],
        quad_y,
        [pltpu.VMEM((rows_z, C), F32)],
        links=at,
        after=[middle, got[0], got[3]],
    )
    piece_bf = ((rows_y, C), BF)
    (part,) = call(k_y_sum, [own, *moves(parts, "y")], [piece_bf])
    grad, mixed, token = call(
        k_input_grad,
        [*got, middle, mixed0, mixed_e],
        [cell_bf, cell_bf, ((8, 128), F32)],
        [WIDE[0], WIDER[2]],
        links=lk,
        after=[part],
        limit=16,
    )
    root = math.sqrt(CELLS * lax.axis_size("lat") * lax.axis_size("tile"))
    (part,) = call(
        functools.partial(k_x_sum, 1.0 / root), [part, *moves([part] * 3, "x")], [piece_bf]
    )
    (part,) = call(
        k_join, [part, *gathers(part, "y")], [((rows_z, C), BF)], links=at, after=[token]
    )
    parts = [part, *gathers(part, "z")]
    others = [move(part, "core", 1) for part in parts]
    buffers = [pltpu.VMEM((4, rows_z, C), F32), pltpu.SemaphoreType.DMA((8,))]
    sums = call(
        k_unpack_own, parts, [cell_f32, cell_f32], buffers, links=at, out_specs=[HBM, HBM],
        after=[parts[0]],
    )
    first, second = call(
        k_unpack_other,
        others,
        [cell_f32, cell_f32],
        buffers,
        links=at,
        hbm=sums,
        alias={5: 0, 6: 1},
        out_specs=[HBM, HBM],
    )
    return (
        mixed.reshape(S, S, C),
        grad.reshape(S, S, C),
        first.reshape(3, 3, C, C),
        second.reshape(3, 3, C, C),
    )


def solution(mesh):
    placed = (P("lat", "tile", None), P("lat", "tile", None), P(), P(), P(), P())
    return jax.shard_map(
        shards,
        mesh=mesh,
        in_specs=placed,
        out_specs=(P("lat", "tile", None), P("lat", "tile", None), P(), P()),
        check_vma=False,
    )
```

```python
import functools
import math

import jax
import jax.numpy as jnp
from jax import lax
from jax.experimental import pallas as pl
from jax.experimental.pallas import tpu as pltpu
from jax.sharding import PartitionSpec as P

S = 48
C = 256
CELLS = S * S
ROWS = 8
BLK = ROWS * S
N_BLK = S // ROWS
HALF = 9 * C // 2
PK = 64
F32 = jnp.float32
BF = jnp.bfloat16
MIB = 1 << 20


def side_slot(lk, s):
    return lk[s * 3]


def side_flip(lk, s):
    return lk[s * 3 + 2]


def corner_slot(lk, c):
    return lk[12 + c * 3]


def corner_keep(lk, c):
    return lk[12 + c * 3 + 2]


def side_facing(lk, slot):
    found = jnp.int32(0)
    for s in range(1, 4):
        found = jnp.where(side_slot(lk, s) == slot, jnp.int32(s), found)
    return found


def flip_facing(lk, slot):
    found = side_flip(lk, 0)
    for s in range(1, 4):
        found = jnp.where(side_slot(lk, s) == slot, side_flip(lk, s), found)
    return found


def corner_facing(lk, slot, values):
    found = values[0]
    for c in range(1, 4):
        found = jnp.where(corner_slot(lk, c) == slot, values[c], found)
    return found


def slot_at(lat_step, tile_step):
    return (lat_step + 1) * 3 + tile_step + 1


def package_slots(lk):
    la, ta = lk[24], lk[25]
    return slot_at(la, 0), slot_at(0, ta), slot_at(0, -ta), slot_at(-la, 0)


def package_corners(lk, q):
    la, ta = lk[24], lk[25]
    if q == 1:
        return slot_at(la, ta), slot_at(-la, ta)
    if q == 2:
        return slot_at(la, -ta), slot_at(-la, -ta)
    return ()


def corner_home(lk, c):
    d = corner_slot(lk, c)
    row = jnp.where(d % 3 - 1 == lk[25], jnp.int32(S), jnp.int32(S + 1))
    return row + jnp.where(d // 3 - 1 == lk[24], jnp.int32(0), jnp.int32(3 * PK))


def side_home(lk, s):
    slots = package_slots(lk)
    home = jnp.int32(3 * PK)
    for q in range(3):
        home = jnp.where(side_slot(lk, s) == slots[q], jnp.int32(q * PK), home)
    return home


def grid_of(rows, cols):
    row = lax.broadcasted_iota(jnp.int32, (rows, cols), 0)
    col = lax.broadcasted_iota(jnp.int32, (rows, cols), 1)
    return row, col


def ones_at(hit):
    return jnp.where(hit, 1.0, 0.0).astype(BF)


def pick(hit, rows):
    return jnp.dot(ones_at(hit), rows, preferred_element_type=F32)


def pack_edges(lk, edges):
    row, col = grid_of(PK, 4 * S)
    at = [jnp.int32(c // 2 * S + c % 2 * (S - 1)) for c in range(4)]
    hits = []
    for q, slot in enumerate(package_slots(lk)):
        want = jnp.where(row < S, side_facing(lk, slot) * S + row, -1)
        for k, far in enumerate(package_corners(lk, q)):
            want = jnp.where(row == S + k, corner_facing(lk, far, at), want)
        hits.append(col == want)
    return pick(jnp.concatenate(hits, axis=0), edges).astype(BF)


def pack_rims(lk, rims):
    row, col = grid_of(PK, 4 * PK)
    at = []
    for c in range(4):
        place = jnp.int32(c // 2 * PK + S + c % 2)
        at.append(jnp.where(corner_keep(lk, c) != 0, place, jnp.int32(-1)))
    hits = []
    for q, slot in enumerate(package_slots(lk)):
        cell = jnp.where(flip_facing(lk, slot) == 1, S - 1 - row, row)
        want = jnp.where(row < S, side_facing(lk, slot) * PK + cell, -1)
        for k, far in enumerate(package_corners(lk, q)):
            want = jnp.where(row == S + k, corner_facing(lk, far, at), want)
        hits.append(col == want)
    return pick(jnp.concatenate(hits, axis=0), rims).astype(BF)


def halo_rows(lk, got):
    row, col = grid_of(S, 4 * PK)
    hits = []
    for s in range(4):
        for t in range(3):
            at = row + (t - 1)
            cell = jnp.where(side_flip(lk, s) == 1, S - 1 - at, at)
            want = jnp.where((at >= 0) & (at < S), side_home(lk, s) + cell, -1)
            if s < 2:
                for end, c in ((-1, 2 * s), (S, 2 * s + 1)):
                    home = jnp.where(corner_keep(lk, c) != 0, corner_home(lk, c), -1)
                    want = jnp.where(at == end, home, want)
            hits.append(col == want)
    cells = pick(jnp.concatenate(hits, axis=0), got).astype(BF)
    taps = [cells[n * S : (n + 1) * S] for n in range(12)]
    return [jnp.concatenate(taps[3 * s : 3 * s + 3], axis=1) for s in range(4)]


def rim_adds(lk, got):
    row, col = grid_of(S, 4 * PK)
    hits = []
    for s in range(4):
        hit = col == side_home(lk, s) + row
        if s < 2:
            for end, c in ((0, 2 * s), (S - 1, 2 * s + 1)):
                hit = hit | ((row == end) & (col == corner_home(lk, c)))
        hits.append(hit)
    adds = pick(jnp.concatenate(hits, axis=0), got)
    return [adds[s * S : (s + 1) * S] for s in range(4)]


def cross(adds):
    top, bottom, left, right = adds
    row = lax.broadcasted_iota(jnp.int32, (S, C), 0)
    first = row == 0
    last = row == S - 1

    def with_ends(base, head, tail):
        return base + jnp.where(first, head, 0.0) + jnp.where(last, tail, 0.0)

    return [
        with_ends(top, left[0:1], right[0:1]),
        with_ends(bottom, left[S - 1 :], right[S - 1 :]),
        with_ends(left, top[0:1], bottom[0:1]),
        with_ends(right, top[S - 1 :], bottom[S - 1 :]),
    ]


def gelu_both(z):
    phi = 0.5 + 0.5 * lax.erf(z * (1.0 / math.sqrt(2.0)))
    dens = jnp.exp(z * z * -0.5) * (1.0 / math.sqrt(2.0 * math.pi))
    return z * phi, phi + z * dens


def dot(a, b):
    return jnp.dot(a, b, preferred_element_type=F32)


def dot_nt(a, b):
    return lax.dot_general(a, b, (((1,), (1,)), ((), ())), preferred_element_type=F32)


def halo_sums(sides, w):
    out = [dot(sides[0], w[0]), dot(sides[1], w[2])]
    for s, b in ((2, 0), (3, 2)):
        total = None
        for a in range(3):
            term = dot(sides[s][:, a * C : (a + 1) * C], w[a, b * C : (b + 1) * C])
            total = term if total is None else total + term
        out.append(total)
    return cross(out)


def rims_of(edges, w):
    row, col = grid_of(PK, 4 * S)
    hits = []
    for s in range(4):
        for t in range(3):
            if s < 2:
                pos = jnp.where(row < S, row + 1, jnp.where(row == S, 0, S + 1))
                used = row < S + 2
            else:
                pos = row + 1
                used = row < S
            src = pos - t
            hits.append(used & (src >= 0) & (src < S) & (col == s * S + src))
    cells = pick(jnp.concatenate(hits, axis=0), edges).astype(BF)
    out = []
    for s in range(4):
        total = None
        for t in range(3):
            a, b = ((0, 2)[s], t) if s < 2 else (t, (0, 2)[s - 2])
            n = 3 * s + t
            term = dot_nt(cells[n * PK : (n + 1) * PK], w[a, b * C : (b + 1) * C])
            total = term if total is None else total + term
        out.append(total.astype(BF))
    return jnp.concatenate(out, axis=0)


def put_edges(x, edges):
    x[pl.ds(0, S)] = edges[pl.ds(0, S)]
    x[pl.ds(CELLS - S, S)] = edges[pl.ds(S, S)]
    for r in range(S):
        x[pl.ds(r * S, 1)] = edges[pl.ds(2 * S + r, 1)]
        x[pl.ds(r * S + S - 1, 1)] = edges[pl.ds(3 * S + r, 1)]


def take_edges(x, edges):
    edges[pl.ds(0, S)] = x[pl.ds(0, S)]
    edges[pl.ds(S, S)] = x[pl.ds(CELLS - S, S)]
    for r in range(S):
        edges[pl.ds(2 * S + r, 1)] = x[pl.ds(r * S, 1)]
        edges[pl.ds(3 * S + r, 1)] = x[pl.ds(r * S + S - 1, 1)]


def spread_columns(x, frame, left, right):
    zero = jnp.zeros((S, 3 * C), BF)
    frame[pl.ds(0, S)] = zero
    frame[pl.ds(CELLS + S, S)] = zero
    row = lax.broadcasted_iota(jnp.int32, (S, C), 0)

    @pl.loop(0, S, unroll=4)
    def _(r):
        cells = x[pl.ds(pl.multiple_of(r * S, S), S)]
        to = pl.ds(pl.multiple_of(r * S + S, S), S)
        before = jnp.where(row == 0, 0.0, pltpu.roll(cells, 1, 0))
        after = jnp.where(row == S - 1, 0.0, pltpu.roll(cells, S - 1, 0))
        frame[to, left * C : (left + 1) * C] = before.astype(BF)
        frame[to, C : 2 * C] = cells.astype(BF)
        frame[to, right * C : (right + 1) * C] = after.astype(BF)


def half(i):
    return pl.ds(pl.multiple_of(i * HALF, HALF), HALF)


def block_of(i):
    return pl.ds(i * BLK, BLK)


def conv_block(frame, w, i):
    total = None
    for a in range(3):
        term = dot(frame[pl.ds(i * BLK + a * S, BLK)], w[a])
        total = term if total is None else total + term
    return total


def back_block(frame, w, i):
    total = None
    for a in range(3):
        at = pl.ds(i * BLK + (2 - a) * S, BLK)
        for b in range(3):
            part = frame[at, b * C : (b + 1) * C]
            term = dot_nt(part, w[a, b * C : (b + 1) * C])
            total = term if total is None else total + term
    return total


def weight_sums(xt, frame, halo, edges, store):
    side = []
    for s in range(4):
        side.append(
            lax.dot_general(
                halo[s * S : (s + 1) * S],
                edges[s * S : (s + 1) * S],
                (((0,), (0,)), ((), ())),
                preferred_element_type=F32,
            )
        )
    for a in range(3):
        whole = dot(xt[...], frame[pl.ds((2 - a) * S, CELLS)])
        for b in range(3):
            part = whole[:, b * C : (b + 1) * C]
            if a == 0:
                part = part + side[0][b * C : (b + 1) * C]
            if a == 2:
                part = part + side[1][b * C : (b + 1) * C]
            if b == 0:
                part = part + side[2][a * C : (a + 1) * C]
            if b == 2:
                part = part + side[3][a * C : (a + 1) * C]
            store((a * 3 + b) * C, part.astype(BF))


def column_of(strip, at):
    row = lax.broadcasted_iota(jnp.int32, (S, 16, C), 1)
    return jnp.sum(jnp.where(row == at, strip.astype(F32), 0.0), axis=1).astype(BF)


def edges_of(field):
    right = column_of(field[:, S - 16 :, :], 15)
    return jnp.concatenate(
        [field[0], field[S - 1], column_of(field[:, 0:16, :], 0), right], axis=0
    )


def k_pack_field(at, side, corner, field, pk, links, cells):
    cells[...] = field[...].reshape(CELLS, C)
    links[24] = 1 - at[3] % 2 * 2
    links[25] = 1 - at[4] % 2 * 2
    for s in range(4):
        for k in range(3):
            links[s * 3 + k] = side[s, k]
            links[12 + s * 3 + k] = corner[s, k]
    pk[...] = pack_edges(links, edges_of(field))


def k_edges(field, after, edges):
    edges[...] = edges_of(field)


def k_second_frame(he, hidden0, frame, xt, x, edges):
    edges[...] = he[...].astype(F32)
    x[...] = hidden0[...].astype(F32)
    put_edges(x, edges)
    xt[...] = x[...].astype(BF).T
    spread_columns(x, frame, 0, 2)


def k_delta_frame(de, delta0, frame, x, edges):
    edges[...] = de[...].astype(F32)
    x[...] = delta0[...].astype(F32)
    put_edges(x, edges)
    spread_columns(x, frame, 2, 0)


def k_first_frame(field, frame, xt, x):
    x[...] = field[...].astype(F32)
    xt[...] = field[...].T
    spread_columns(x, frame, 0, 2)


def k_first(frame, w, after, hidden, slope, e0, x):
    for i in range(N_BLK):
        to = block_of(i)
        z = conv_block(frame, w, i)
        x[to] = z
        value, grad = gelu_both(z)
        hidden[to] = value.astype(BF)
        slope[to] = grad

    take_edges(x, e0)


def join(got):
    return jnp.concatenate([g[...] for g in got], axis=0)


def k_first_edges(lk, up, left, right, down, e0, w, halo, slope, hidden, pk):
    sides = halo_rows(lk, join((up, left, right, down)))
    for s in range(4):
        halo[pl.ds(s * S, S)] = sides[s]
    z = e0[...] + jnp.concatenate(halo_sums(sides, w), axis=0)
    value, grad = gelu_both(z)
    slope[...] = grad
    hidden[...] = value.astype(BF)
    pk[...] = pack_edges(lk, value.astype(BF))


def k_second(frame, cot, w, after, mixed, delta, e0, x):
    for i in range(N_BLK):
        to = block_of(i)
        z = conv_block(frame, w, i)
        x[to] = z
        value, grad = gelu_both(z)
        mixed[to] = value.astype(BF)
        delta[to] = (cot[to].astype(F32) * grad).astype(BF)

    take_edges(x, e0)


def k_second_edges(lk, up, left, right, down, e0, ec, w, halo, mixed, delta, pk):
    sides = halo_rows(lk, join((up, left, right, down)))
    for s in range(4):
        halo[pl.ds(s * S, S)] = sides[s]
    z = e0[...] + jnp.concatenate(halo_sums(sides, w), axis=0)
    value, grad = gelu_both(z)
    mixed[...] = value.astype(BF)
    edges = (ec[...].astype(F32) * grad).astype(BF)
    delta[...] = edges
    pk[...] = pack_rims(lk, rims_of(edges, w))


def k_second_back(
    at, de, halo, frame, w, xt, slope, after, keep, send, fd, e0, x, tv
):
    for i in range(N_BLK):
        to = block_of(i)
        g = back_block(frame, w, i)
        x[to] = g
        fd[to] = (g * slope[to]).astype(BF)

    take_edges(x, e0)

    def store(row, part):
        tv[pl.ds(row, C)] = part

    weight_sums(xt, frame, halo, de, store)
    keep[...] = tv[half(at[0])]
    send[...] = tv[half(1 - at[0])]


def k_first_delta_edges(lk, up, left, right, down, e0, slope, w, delta, pk):
    adds = cross(rim_adds(lk, join((up, left, right, down))))
    grad = e0[...] + jnp.concatenate(adds, axis=0)
    edges = (grad * slope[...]).astype(BF)
    delta[...] = edges
    pk[...] = pack_rims(lk, rims_of(edges, w))


def half_sums(h, xt, frame, side, out):
    for n in range(4):
        tap = h * 5 + n
        a, b = tap // 3, tap % 3
        rows = pl.ds(pl.multiple_of((2 - a) * S, 16), CELLS)
        lanes = pl.ds(pl.multiple_of(b * C, C), C)
        part = dot(xt[...], frame[rows, lanes])
        part = part + side[pl.ds(pl.multiple_of(tap * C, C), C)]
        out[pl.ds(pl.multiple_of(n * C + h * (C // 2), C // 2), C)] = part.astype(BF)
    part = dot(xt[pl.ds(pl.multiple_of(h * (C // 2), C // 2), C // 2)], frame[pl.ds(S, CELLS), C : 2 * C])
    out[pl.ds(pl.multiple_of((1 - h) * 4 * C, C), C // 2)] = part.astype(BF)


def k_first_send(at, de, halo, delta0, xt, send, frame, side, x, edges):
    edges[...] = de[...].astype(F32)
    x[...] = delta0[...].astype(F32)
    put_edges(x, edges)
    spread_columns(x, frame, 2, 0)
    terms = [
        lax.dot_general(
            halo[s * S : (s + 1) * S],
            de[s * S : (s + 1) * S],
            (((0,), (0,)), ((), ())),
            preferred_element_type=F32,
        )
        for s in range(4)
    ]
    for a in range(3):
        for b in range(3):
            total = None
            for s, used, n in ((0, a == 0, b), (1, a == 2, b), (2, b == 0, a), (3, b == 2, a)):
                if used:
                    term = terms[s][n * C : (n + 1) * C]
                    total = term if total is None else total + term
            if total is not None:
                side[pl.ds((a * 3 + b) * C, C)] = total
    half_sums(1 - at[0], xt, frame, side, send)


def k_first_keep(at, xt, frame, side, keep):
    half_sums(at[0], xt, frame, side, keep)


def k_input_middle(de, delta0, w, after, out, x, frame, edges):
    x[...] = delta0[...].astype(F32)
    edges[...] = de[...].astype(F32)
    put_edges(x, edges)
    spread_columns(x, frame, 2, 0)

    for i in range(N_BLK):
        out[block_of(i)] = back_block(frame, w, i)


def k_input_grad(lk, up, left, right, down, middle, mixed0, me, after, out, mixed, token, x, edges):
    adds = cross(rim_adds(lk, join((up, left, right, down))))
    x[...] = middle[...]
    take_edges(x, edges)
    edges[...] += jnp.concatenate(adds, axis=0)
    put_edges(x, edges)
    out[...] = x[...].astype(BF)
    x[...] = mixed0[...].astype(F32)
    edges[...] = me[...].astype(F32)
    put_edges(x, edges)
    mixed[...] = x[...].astype(BF)
    token[...] = jnp.zeros_like(token)


STEPS = (0, 1, 3, 2)


def quarter(place, step, rows):
    return pl.ds(pl.multiple_of((place ^ step) * rows, 16), rows)


def k_core_sum(at, keep1, got1, keep2, got2, pk, own, s1, s3, s2, pk_out):
    rows = own.shape[0] // 2
    for step, out in zip(STEPS, (own, s1, s3, s2)):
        part = quarter(at[1], step, rows)
        for k, (keep, got) in enumerate(((keep1, got1), (keep2, got2))):
            total = keep[part].astype(F32) + got[part].astype(F32)
            out[pl.ds(k * rows, rows)] = total.astype(out.dtype)
    pk_out[...] = pk[...]


def k_z_sum(at, own, g2, g3, g1, *refs):
    o, s1, s3, s2, x = refs[-5:]
    rows = o.shape[0]
    x[...] = (own[...] + g2[...].astype(F32)) + (g1[...].astype(F32) + g3[...].astype(F32))
    for step, out in zip(STEPS, (o, s1, s3, s2)):
        out[...] = x[quarter(at[2], step, rows)].astype(out.dtype)


def k_y_sum(own, g1, g3, g2, out):
    total = (own[...] + g2[...].astype(F32)) + (g1[...].astype(F32) + g3[...].astype(F32))
    out[...] = total.astype(BF)


def k_x_sum(scale, own, g1, g3, g2, out):
    total = (own[...].astype(F32) + g2[...].astype(F32)) + (
        g1[...].astype(F32) + g3[...].astype(F32)
    )
    out[...] = (total * scale).astype(BF)


def k_join(at, own, g1, g3, g2, after, out):
    rows = own.shape[0]
    for step, part in zip(STEPS, (own, g1, g3, g2)):
        out[quarter(at[2], step, rows)] = part[...]


def unpack(core, at, parts, first, second, buf, sems):
    rows = HALF // 4
    copies = []
    for q, (step, part) in enumerate(zip(STEPS, parts)):
        place = core * HALF + (at[1] ^ step) * rows
        to = pl.ds(pl.multiple_of(place, 16), rows)
        buf[q] = part[...].astype(F32)
        for k, out in enumerate((first, second)):
            copy = pltpu.make_async_copy(
                buf.at[q, pl.ds(k * rows, rows)], out.at[to], sems.at[2 * q + k]
            )
            copy.start()
            copies.append(copy)
    for copy in copies:
        copy.wait()


def k_unpack_own(at, a0, a1, a3, a2, after, first, second, buf, sems):
    unpack(at[0], at, (a0, a1, a3, a2), first, second, buf, sems)


def k_unpack_other(at, b0, b1, b3, b2, first_in, second_in, first, second, buf, sems):
    unpack(1 - at[0], at, (b0, b1, b3, b2), first, second, buf, sems)


VMEM = pl.BlockSpec(memory_space=pltpu.VMEM)
SMEM = pl.BlockSpec(memory_space=pltpu.SMEM)
ANY = pl.BlockSpec(memory_space=pl.ANY)
HBM = pl.BlockSpec(memory_space=pltpu.HBM)
CELL_BF = pltpu.VMEM((CELLS, C), BF)
WIDE = [pltpu.VMEM((CELLS, C), F32), pltpu.VMEM((CELLS + 2 * S, 3 * C), BF)]
WIDER = WIDE + [pltpu.VMEM((4 * S, C), F32)]


def call(kernel, args, outs, scratch=(), links=None, flops=0, after=(), limit=8, hbm=(), alias=None, out_specs=None):
    given = ([links] if links is not None else []) + [*args, *hbm, *after]
    specs = ([SMEM] if links is not None else []) + [VMEM] * len(args)
    specs += [HBM] * len(hbm) + [ANY] * len(after)
    name = getattr(kernel, "__name__", None) or kernel.func.__name__
    return pl.pallas_call(
        kernel,
        out_shape=[
            (pltpu.VMEM if len(out) > 2 else jax.ShapeDtypeStruct)(out[0], out[1]) for out in outs
        ],
        in_specs=specs,
        out_specs=out_specs or [VMEM] * len(outs),
        input_output_aliases=alias or {},
        scratch_shapes=list(scratch),
        compiler_params=pltpu.CompilerParams(vmem_limit_bytes=limit * MIB),
        cost_estimate=pl.CostEstimate(
            flops=int(flops), bytes_accessed=4 * MIB, transcendentals=0
        ),
        name=name,
    )(*given)


def pairs_a(count):
    return [(i, i ^ 1) for i in range(count)]


def pairs_b(count):
    return [(i, (i + 1 if i % 2 else i - 1) % count) for i in range(count)]


def trade_tile(pk):
    n = lax.axis_size("tile")
    from_a = lax.ppermute(pk[PK : 2 * PK], "tile", pairs_a(n))
    from_b = lax.ppermute(pk[2 * PK : 3 * PK], "tile", pairs_b(n))
    return from_a, from_b


def trade_lat(to_a, to_b):
    n = lax.axis_size("lat")
    return lax.ppermute(to_a, "lat", pairs_a(n)), lax.ppermute(to_b, "lat", pairs_b(n))


def trade(pk):
    tile_a, tile_b = trade_tile(pk)
    filler = jnp.zeros((PK - S - 2, C), BF)

    def with_cells(edge, k):
        cells = [tile_a[S + k : S + k + 1], tile_b[S + k : S + k + 1]]
        return jnp.concatenate([edge[:S], *cells, filler], axis=0)

    lat_a, lat_b = trade_lat(with_cells(pk[:PK], 0), with_cells(pk[3 * PK :], 1))
    return lat_a, tile_a, tile_b, lat_b


def exchange(kind, step):
    pairs = []
    for t in range(16):
        for l in range(8):
            y, xl, c, xh, z = t // 4, t // 2 % 2, t % 2, l // 4, l % 4
            x = xh * 2 + xl
            if kind == "core":
                c ^= step
            elif kind == "z":
                z ^= step
            elif kind == "y":
                y ^= step
            else:
                x ^= step
            to = (y * 4 + x % 2 * 2 + c) * 8 + x // 2 * 4 + z
            pairs.append((t * 8 + l, to))
    return pairs


def move(x, kind, step):
    return lax.ppermute(x, ("tile", "lat"), exchange(kind, step))


def moves(parts, kind):
    return [move(part, kind, step) for part, step in zip(parts, STEPS[1:])]


def gathers(part, kind):
    return [move(part, kind, step) for step in STEPS[1:]]


def shards(field, cotangent, first_weight, second_weight, side_links, corner_links):
    lat_at = lax.axis_index("lat")
    lon_at = lax.axis_index("tile")
    core, z_at, y_at = lon_at % 2, lat_at % 4, lon_at // 4
    at = jnp.stack([core, z_at, y_at, lat_at, lon_at]).astype(jnp.int32)
    w1 = first_weight.reshape(3, 3 * C, C)
    w2 = second_weight.reshape(3, 3 * C, C)
    cot = cotangent.reshape(CELLS, C)
    cell_bf, cell_f32 = ((CELLS, C), BF), ((CELLS, C), F32)
    edge_bf, edge_f32 = ((4 * S, C), BF), ((4 * S, C), F32)
    halo_bf, turned, packs = ((4 * S, 3 * C), BF), ((C, CELLS), BF), ((4 * PK, C), BF)
    work = 2 * CELLS * 9 * C * C

    far_bf, far_f32 = ((CELLS, C), BF, 1), ((CELLS, C), F32, 1)
    far_turned = ((C, CELLS), BF, 1)

    frame_bf = ((CELLS + 2 * S, 3 * C), BF, 1)
    half_bf = ((HALF, C), BF)

    own_side = side_links[lat_at, lon_at]
    own_corner = corner_links[lat_at, lon_at]
    pk, lk, cells = pl.pallas_call(
        k_pack_field,
        out_shape=[jax.ShapeDtypeStruct(*packs), jax.ShapeDtypeStruct((26,), jnp.int32), pltpu.VMEM((CELLS, C), BF)],
        in_specs=[SMEM, SMEM, SMEM, VMEM],
        out_specs=[VMEM, SMEM, VMEM],
        compiler_params=pltpu.CompilerParams(vmem_limit_bytes=8 * MIB),
        name="k_pack_field",
    )(at, own_side, own_corner, field)
    got = trade(pk)
    frame, xt1 = call(k_first_frame, [cells], [frame_bf, far_turned], WIDE[:1], limit=12)
    (cot_e,) = call(k_edges, [cotangent], [edge_bf], after=[got[1]])
    hidden0, slope0, e0 = call(
        k_first,
        [frame, w1],
        [far_bf, far_f32, edge_f32],
        WIDE[:1],
        after=[got[1]],
        flops=work,
        limit=18,
    )
    halo1, slope_e, hidden_e, pk = call(
        k_first_edges, [*got, e0, w1], [halo_bf, edge_f32, edge_bf, packs], links=lk
    )
    got = trade(pk)
    frame, xt2 = call(
        k_second_frame, [hidden_e, hidden0], [frame_bf, far_turned], [WIDE[0], WIDER[2]], limit=14
    )
    mixed0, delta0, e0 = call(
        k_second,
        [frame, cot, w2],
        [far_bf, far_bf, edge_f32],
        WIDE[:1],
        after=[got[1]],
        flops=work,
        limit=18,
    )
    halo2, mixed_e, delta_e, pk = call(
        k_second_edges, [*got, e0, cot_e, w2], [halo_bf, edge_bf, edge_bf, packs], links=lk
    )
    got = trade(pk)
    (frame,) = call(
        k_delta_frame, [delta_e, delta0], [frame_bf], [WIDE[0], WIDER[2]], limit=12
    )
    keep2, send2, fd0, e0 = call(
        k_second_back,
        [delta_e, halo2, frame, w2, xt2, slope0],
        [half_bf, half_bf, far_bf, edge_f32],
        [WIDE[0], CELL_BF],
        links=at,
        after=[got[1]],
        flops=2 * work,
        limit=22,
    )
    got2 = move(send2, "core", 1)
    fd_e, pk = call(
        k_first_delta_edges, [*got, e0, slope_e, w1], [edge_bf, packs], links=lk
    )
    send1, frame, side = call(
        k_first_send,
        [fd_e, halo1, fd0, xt1],
        [half_bf, frame_bf, ((9 * C, C), F32, 1)],
        [WIDE[0], WIDER[2]],
        links=at,
        flops=work,
        limit=20,
    )
    got1 = move(send1, "core", 1)
    (keep1,) = call(
        k_first_keep, [xt1, frame, side], [half_bf], links=at, flops=work, limit=14
    )
    rows_z, rows_y = CELLS // 4, CELLS // 16
    quad_z = [((rows_z, C), F32)] + [((rows_z, C), BF)] * 3
    own, *parts, pk = call(
        k_core_sum, [keep1, got1, keep2, got2, pk], quad_z + [packs], links=at
    )
    got = trade(pk)
    (middle,) = call(
        k_input_middle, [fd_e, fd0, w1], [cell_f32], WIDER, flops=work, after=[got[1]], limit=18
    )
    quad_y = [((rows_y, C), F32)] + [((rows_y, C), BF)] * 3
    own, *parts = call(
        k_z_sum,
        [own, *moves(parts, "z")[::-1]],
        quad_y,
        [pltpu.VMEM((rows_z, C), F32)],
        links=at,
        after=[middle, got[0], got[3]],
    )
    piece_bf = ((rows_y, C), BF)
    (part,) = call(k_y_sum, [own, *moves(parts, "y")], [piece_bf])
    grad, mixed, token = call(
        k_input_grad,
        [*got, middle, mixed0, mixed_e],
        [cell_bf, cell_bf, ((8, 128), F32)],
        [WIDE[0], WIDER[2]],
        links=lk,
        after=[part],
        limit=16,
    )
    root = math.sqrt(CELLS * lax.axis_size("lat") * lax.axis_size("tile"))
    (part,) = call(
        functools.partial(k_x_sum, 1.0 / root), [part, *moves([part] * 3, "x")], [piece_bf]
    )
    (part,) = call(
        k_join, [part, *gathers(part, "y")], [((rows_z, C), BF)], links=at, after=[token]
    )
    parts = [part, *gathers(part, "z")]
    others = [move(part, "core", 1) for part in parts]
    buffers = [pltpu.VMEM((4, rows_z, C), F32), pltpu.SemaphoreType.DMA((8,))]
    sums = call(
        k_unpack_own, parts, [cell_f32, cell_f32], buffers, links=at, out_specs=[HBM, HBM],
        after=[parts[0]],
    )
    first, second = call(
        k_unpack_other,
        others,
        [cell_f32, cell_f32],
        buffers,
        links=at,
        hbm=sums,
        alias={5: 0, 6: 1},
        out_specs=[HBM, HBM],
    )
    return (
        mixed.reshape(S, S, C),
        grad.reshape(S, S, C),
        first.reshape(3, 3, C, C),
        second.reshape(3, 3, C, C),
    )


def solution(mesh):
    placed = (P("lat", "tile", None), P("lat", "tile", None), P(), P(), P(), P())
    return jax.shard_map(
        shards,
        mesh=mesh,
        in_specs=placed,
        out_specs=(P("lat", "tile", None), P("lat", "tile", None), P(), P()),
        check_vma=False,
    )
```
